256 devices in a mesh: tp: 16 (over z, core), ep: 16 (over y, x).
Axes of the slice: x: 4, y: 4, z: 8, core: 2. Of those that a mesh axis runs over, the one named last changes fastest.
Arguments:
- context: bfloat16 [4096, 4096], P('ep', 'tp'), may hold values from -6 to 6
- out_weight: bfloat16 [4096, 4096], P('tp'), may hold values from -0.125 to 0.125
- residual: bfloat16 [4096, 4096], P('ep', 'tp'), may hold values from -20 to 20
- norm_gain: bfloat16 [4096], replicated, may hold values from 0.099609375 to 1.8984375
- router_weight: bfloat16 [64, 4096], replicated, may hold values from -0.09375 to 0.09375
- expert_ids: int32 [4096, 8], P('ep'), may hold values from 0 to 63, all different within a row; in each aligned block of 256 rows (0 to 255, 256 to 511, ...) at most 64 rows name the same one
- w_gate: bfloat16 [256, 4096, 384], P(('tp', 'ep')), may hold values from -0.09375 to 0.09375
- w_up: bfloat16 [256, 4096, 384], P(('tp', 'ep')), may hold values from -0.09375 to 0.09375
- w_down: bfloat16 [256, 384, 4096], P(('tp', 'ep')), may hold values from -0.15625 to 0.15625
Outputs:
- layer_out: bfloat16 [4096, 4096], P('ep', 'tp')
The draws below stay inside these ranges and needn't reach their ends.
Inputs may be any that keep to these rules, and one draw needn't show every extreme that they name: `expert_ids`: each row names 8 different experts. In each aligned block of 256 rows (the rows of one index of ep) no expert is named by more than 64 rows, a bound that some block reaches.
All inputs are finite; a program needn't handle non-finite values.
Results may differ from the reference program's by a relative error of at most 0.008.
Values may be sent and summed in bfloat16 or wider, within the bound.
A program may use at most 128 MiB of HBM per device.

```python
import math
import jax
import jax.numpy as jnp
import numpy as np
from jax import lax

D = 4096
HEADS = 32
HEAD_DIM = 128
FF = 1536
TOP = 8
SPLIT = 4
TOKENS_EP = 256
TOKENS = 4096
EXPERTS = 64
FFS = 384
CAP = 64
N_EP = 16


def draw_residual(key, part):
    key = jax.random.fold_in(key, 11)
    key_noise, key_rows = jax.random.split(key, 2)
    column = jnp.arange(D, dtype=jnp.float32) / (D - 1)
    row_scale = jnp.exp(jax.random.uniform(key_rows, (TOKENS, 1), jnp.float32, jnp.log(0.4), jnp.log(4.0)))
    noise = jnp.clip(jax.random.normal(key_noise, (TOKENS, D), jnp.float32), -5.0, 5.0)
    col_scale = 0.1 * jnp.exp(jnp.log(10.0) * column)
    drawn = noise * col_scale * row_scale
    return drawn.astype(jnp.bfloat16)


def with_spikes(entries, key, source, target, parts, factor):
    def block_of(axis_at):
        return (jnp.arange(entries.shape[axis_at]) // (entries.shape[axis_at] // parts)).reshape((-1,) + (1,) * (entries.ndim - 1 - axis_at))

    near = jax.random.permutation(key, parts)[block_of(target)]
    second = (block_of(target) + parts // 2) % parts
    return jnp.where((block_of(source) == near) | (block_of(source) == second), factor * entries, entries)


def steps_of(rng, extent, pieces, low, largest):
    def one(axis_at, shards_of):
        draws = jax.random.uniform(jax.random.fold_in(jax.random.fold_in(rng, 6), axis_at), (shards_of,), jnp.float32, low / len(pieces), largest / len(pieces))
        return jnp.repeat(jnp.exp(draws), extent[axis_at] // shards_of).reshape((-1,) + (1,) * (len(extent) - axis_at - 1))

    factor_of = one(*pieces[0])
    for cut in pieces[1:]:
        factor_of = factor_of * one(*cut)
    return factor_of


def routed_block(stream_key, own, number, rows, number_of, top, bound, lean):
    sequence = jax.random.permutation(stream_key, number_of)
    heavy_load, ordinary = portions_of(number_of, rows * top, bound, lean, True), portions_of(number_of, rows * top, bound, lean, False)
    places = jnp.arange(number_of)

    def named(sizes, offset_by):
        used = int((sizes > 0).sum())
        fixed = max(1, used // 4)
        shifted = fixed + (places - fixed + offset_by * (used - fixed)) % max(1, number_of - fixed)
        return jnp.zeros((number_of,), jnp.int32).at[sequence[jnp.where(places < fixed, places, shifted)]].set(jnp.asarray(sizes, jnp.int32))

    sizes = jnp.where(number % 4 == 0, named(heavy_load, number // 4), named(ordinary, number - number // 4 - 1))
    mixed = jax.random.permutation(jax.random.fold_in(own, 3), number_of)
    giver, receiver = mixed[0:number_of // 2 * 2:2], mixed[1:number_of // 2 * 2:2]
    slack = jnp.minimum(sizes[giver] - 1, bound - sizes[receiver]) // 2
    slack = jnp.where((giver == sequence[0]) | (receiver == sequence[0]) | (sizes[receiver] == 0), 0, jnp.maximum(slack, 0))
    shifted = jax.random.randint(jax.random.fold_in(own, 4), (number_of // 2,), 0, 1 << 20) % (slack + 1)
    sizes = sizes.at[giver].add(-shifted).at[receiver].add(shifted)
    items = jnp.searchsorted(jnp.cumsum(sizes), jnp.arange(rows * top), side="right").astype(jnp.int32)
    listing = items.reshape(top, rows).T
    listing = listing[jax.random.permutation(jax.random.fold_in(own, 1), rows)]
    offset_by = jax.random.randint(jax.random.fold_in(own, 2), (rows, 1), 0, top)
    return jnp.take_along_axis(listing, (jnp.arange(top)[None, :] + offset_by) % top, axis=1)


def portions_of(count, total, bound, slope, full):
    portions = [(1 << 20) // math.isqrt(grade ** slope) + 1 for grade in range(1, count + 1)]
    largest = bound if full else min(bound, max(-(-total // count), total * portions[0] // sum(portions)))
    least = 1 if total - largest >= count - 1 else 0
    given, surplus = [largest] + [least] * (count - 1), total - largest - least * (count - 1)
    while surplus > 0:
        free = [i for i in range(1, count) if given[i] < largest] or [i for i in range(1, count) if given[i] < bound]
        mass, remaining = sum([portions[i] for i in free]), surplus
        for i in free:
            more = min(bound - given[i], max(1, remaining * portions[i] // mass), surplus)
            given[i] = given[i] + more
            surplus = surplus - more
    return np.array(given)


def centred(key, dims, scale, reach, cuts=(), held_as=jnp.bfloat16):
    values = jax.random.normal(key, dims, jnp.float32) * scale
    if len(cuts) > 0:
        values = steps_of(key, dims, cuts, -0.22, 0.18) * values
    return jnp.clip(values, min=-reach, max=reach).astype(held_as)


def noise_with(key, dims, width, bound, shards, heavy, kind=jnp.bfloat16):
    result = width * jax.random.normal(key, dims, jnp.float32)
    if shards:
        result = result * steps_of(key, dims, shards, -0.22, 0.18)
    return jnp.clip(with_spikes(result, jax.random.fold_in(key, 3), *heavy), -bound, bound).astype(kind)


def setup_inputs(seed: int = 0) -> dict:
    streams_of = jax.random.split(jax.random.key(seed), 10)
    context = centred(streams_of[0], (TOKENS, HEADS * HEAD_DIM), 1.0, 6.0, ((0, 16), (1, 16)))
    out_weight = noise_with(streams_of[1], (HEADS * HEAD_DIM, D), (HEADS * HEAD_DIM) ** -0.5, 0.125, ((0, 16),), (0, 1, 16, 2.0))
    residual = draw_residual(jax.random.fold_in(streams_of[9], 71), 0)
    norm_gain = jnp.clip(1.0 + 0.18 * jax.random.normal(streams_of[3], (D,), jnp.float32), 0.099609375, 1.8984375).astype(jnp.bfloat16)
    router_weight = centred(streams_of[4], (EXPERTS, D), D ** -0.5, 0.09375)
    expert_ids_keys = jax.random.split(jax.random.fold_in(streams_of[5], 1), TOKENS // TOKENS_EP)
    expert_ids_turns = jax.random.permutation(jax.random.fold_in(streams_of[5], 3), TOKENS // TOKENS_EP)
    expert_ids = jax.vmap(lambda own, number: routed_block(jax.random.fold_in(streams_of[5], 2), own, number, TOKENS_EP, EXPERTS, TOP, CAP, 2))(expert_ids_keys, expert_ids_turns).reshape((TOKENS, TOP))
    w_gate = centred(streams_of[6], (EXPERTS * SPLIT, D, FFS), D ** -0.5, 0.09375, ((0, 256),))
    w_up = centred(streams_of[7], (EXPERTS * SPLIT, D, FFS), D ** -0.5, 0.09375, ((0, 256),))
    w_down = centred(streams_of[8], (EXPERTS * SPLIT, FFS, D), FF ** -0.5, 0.15625, ((0, 256),))
    return {"context": context, "out_weight": out_weight, "residual": residual, "norm_gain": norm_gain, "router_weight": router_weight, "expert_ids": expert_ids, "w_gate": w_gate, "w_up": w_up, "w_down": w_down}


epsilon = 1e-06

def reference(context, out_weight, residual, norm_gain, router_weight, expert_ids, w_gate, w_up, w_down):
    attended = jnp.dot(context, out_weight, preferred_element_type=jnp.float32)
    rounded = lax.optimization_barrier((attended + residual.astype(jnp.float32)).astype(jnp.bfloat16))
    state_float = rounded.astype(jnp.float32)
    inv_rms = lax.rsqrt(lax.optimization_barrier(jnp.mean(state_float * state_float, axis=1, keepdims=True)) + epsilon)
    normed = (state_float * inv_rms * norm_gain.astype(jnp.float32)).astype(jnp.bfloat16)
    logits = jnp.dot(normed, router_weight.T, preferred_element_type=jnp.float32)
    chosen = jnp.take_along_axis(logits, expert_ids, axis=1)
    route_gates = jax.nn.softmax(chosen, axis=1)
    limit = min(TOKENS, N_EP * CAP)
    padded_rows = jnp.concatenate([normed, jnp.zeros((1, D), jnp.bfloat16)], axis=0)
    gate_stack = w_gate.reshape(EXPERTS, SPLIT, D, FFS)
    up_stack = w_up.reshape(EXPERTS, SPLIT, D, FFS)
    down_stack = w_down.reshape(EXPERTS, SPLIT, FFS, D)

    def one_expert(mixture_acc, inputs):
        expert, gate_matrix, up_matrix, down_matrix = inputs
        route_hit = expert_ids == expert
        weight = lax.optimization_barrier(jnp.sum(jnp.where(route_hit, route_gates, 0.0), axis=1))
        routed = jnp.any(route_hit, axis=1)
        row_index = jnp.nonzero(routed, size=limit, fill_value=TOKENS)[0].astype(jnp.int32)
        arrivals = padded_rows[row_index]
        combined = jnp.zeros((limit, D), jnp.float32)
        for slice_id in range(SPLIT):
            gate_act = jnp.dot(arrivals, gate_matrix[slice_id], preferred_element_type=jnp.float32)
            up_act = jnp.dot(arrivals, up_matrix[slice_id], preferred_element_type=jnp.float32)
            inner = (jax.nn.silu(gate_act) * up_act).astype(jnp.bfloat16)
            piece = jnp.dot(inner, down_matrix[slice_id], preferred_element_type=jnp.float32).astype(jnp.bfloat16)
            combined = combined + piece.astype(jnp.float32)
        weight_pad = jnp.concatenate([weight, jnp.zeros((1,), weight.dtype)])
        mixture_acc = mixture_acc.at[row_index].add(weight_pad[row_index][:, None] * combined)
        return (mixture_acc, None)
    start = jnp.zeros((TOKENS + 1, D), jnp.float32)
    experts_list = jnp.arange(EXPERTS, dtype=jnp.int32)
    mixture_acc, unused_out = lax.scan(one_expert, start, (experts_list, gate_stack, up_stack, down_stack))
    return (state_float + mixture_acc[:TOKENS]).astype(jnp.bfloat16)
```

```python
import functools

import jax
import jax.numpy as jnp
from jax import lax
from jax.experimental import pallas as pl
from jax.experimental.pallas import tpu as pltpu
from jax.sharding import PartitionSpec as P

SPLIT = 4
RING = 4
epsilon = 1e-06
MESH = pl.DeviceIdType.MESH
F32 = jnp.float32
BF16 = jnp.bfloat16
VMEM_BYTES = 58 * 2**20
DISTANCES = (4, 3, 5, 2, 6, 1, 7, 0)


def in_vmem(count):
    return [pl.BlockSpec(memory_space=pltpu.VMEM)] * count


def columns(index, width):
    return pl.ds(pl.multiple_of(index * width, width), width)


def greet(devices):
    barrier = pltpu.get_barrier_semaphore()
    for device in devices:
        pl.semaphore_signal(barrier, inc=1, device_id=device, device_id_type=MESH)
    pl.semaphore_wait(barrier, len(devices))


def remote(source, target, send, recv, device):
    return pltpu.make_async_remote_copy(
        src_ref=source, dst_ref=target, send_sem=send, recv_sem=recv, device_id=device, device_id_type=MESH
    )


def tp_place():
    tp, ep = lax.axis_index("tp"), lax.axis_index("ep")
    chips = lax.axis_size("tp") // 2
    z, core = tp // 2, tp % 2
    partner = (z * 2 + 1 - core, ep)
    right = (((z + 1) % chips) * 2 + core, ep)
    left = (((z + chips - 1) % chips) * 2 + core, ep)
    return z, core, chips, partner, right, left


def sum_scratch(rows, width):
    block = (rows, width)
    return [
        pltpu.VMEM((8, *block), BF16),
        pltpu.VMEM((8, *block), BF16),
        pltpu.VMEM((2, 4, *block), BF16),
        pltpu.VMEM((2, 4, *block), BF16),
        pltpu.SemaphoreType.DMA((8,)),
        pltpu.SemaphoreType.DMA((8,)),
        pltpu.SemaphoreType.DMA((2, 4)),
        pltpu.SemaphoreType.DMA((2, 4)),
    ]


def sum_over_tp(term, scratch):
    swap_out, swap_in, arm_out, arm_in, swap_send, swap_recv, arm_send, arm_recv = scratch
    z, core, chips, partner, right, left = tp_place()
    half = swap_out.shape[1] // 2
    whole = pl.ds(0, 2 * half)
    parts = (pl.ds(0, half), pl.ds(half, half))
    swaps = []
    for j in DISTANCES:
        block = ((z + j) % chips) * 2 + 1 - core
        swap_out[j] = term(block).astype(BF16)
        copy = remote(swap_out.at[j], swap_in.at[j], swap_send.at[j], swap_recv.at[j], partner)
        copy.start()
        swaps.append(copy)
    swaps = dict(zip(DISTANCES, swaps))

    def pair(j):
        mine = term(((z + j) % chips) * 2 + core)
        swaps[j].wait_recv()
        return mine + swap_in[j].astype(F32)

    sent = []

    def pass_on(arm, step, span):
        copy = remote(
            arm_out.at[arm, step, span],
            arm_in.at[arm, step, span],
            arm_send.at[arm, step],
            arm_recv.at[arm, step],
            (right, left)[arm],
        )
        copy.start()
        sent.append(copy)
        return copy

    far = pair(4)
    last = [None, None]
    for arm in range(2):
        arm_out[arm, 0, parts[arm]] = far[arm * half : (arm + 1) * half].astype(BF16)
        last[arm] = pass_on(arm, 0, parts[arm])
    for step in range(1, 4):
        for arm in range(2):
            mine = pair(4 - step if arm == 0 else 4 + step)
            last[arm].wait_recv()
            if step == 1:
                arm_out[arm, step] = mine.astype(BF16)
                span = parts[arm]
                came = arm_in[arm, 0, span].astype(F32)
                arm_out[arm, step, span] = (mine[arm * half : (arm + 1) * half] + came).astype(BF16)
            else:
                arm_out[arm, step] = (mine + arm_in[arm, step - 1].astype(F32)).astype(BF16)
            last[arm] = pass_on(arm, step, whole)
    total = pair(0)
    for arm in range(2):
        last[arm].wait_recv()
        total = total + arm_in[arm, 3].astype(F32)
    for copy in sent:
        copy.wait_send()
    for j in DISTANCES:
        swaps[j].wait_send()
    return total


def gather_over_tp(out, width, sems):
    right_send, right_recv, left_send, left_recv, near_send, near_recv = sems
    z, core, chips, partner, right, left = tp_place()
    half = out.shape[0] // 2
    whole = pl.ds(0, 2 * half)
    parts = (pl.ds(0, half), pl.ds(half, half))

    def at(j, span, side):
        return out.at[span, columns(((z + j + chips) % chips) * 2 + side, width)]

    copies = []

    def go(j, span, send, recv, device):
        ref = at(j, span, core)
        copy = remote(ref, ref, send, recv, device)
        copy.start()
        copies.append(copy)

    go(0, whole, right_send.at[0], right_recv.at[0], right)
    go(0, whole, left_send.at[0], left_recv.at[0], left)
    go(0, whole, near_send.at[0], near_recv.at[0], partner)
    for step in range(1, 5):
        span_r = parts[0] if step == 4 else whole
        span_l = parts[1] if step == 4 else whole
        ref = at(-step, span_r, core)
        remote(ref, ref, right_send.at[step - 1], right_recv.at[step - 1], right).wait_recv()
        if step < 4:
            go(-step, parts[0] if step == 3 else whole, right_send.at[step], right_recv.at[step], right)
            go(-step, whole, near_send.at[step], near_recv.at[step], partner)
        ref = at(step, span_l, core)
        remote(ref, ref, left_send.at[step - 1], left_recv.at[step - 1], left).wait_recv()
        if step < 4:
            go(step, parts[1] if step == 3 else whole, left_send.at[step], left_recv.at[step], left)
            go(step, whole, near_send.at[8 - step], near_recv.at[8 - step], partner)
    go(4, whole, near_send.at[4], near_recv.at[4], partner)
    for j in range(8):
        ref = at(-j, whole, 1 - core)
        remote(ref, ref, near_send.at[j], near_recv.at[j], partner).wait_recv()
    for copy in copies:
        copy.wait_send()


def attend_kernel(context, weight, residual, down, hidden, spread, *scratch):
    total_scratch, gather_sems, (spread_send, spread_recv) = scratch[:8], scratch[8:14], scratch[14:16]
    width = residual.shape[1]
    tp, ep = lax.axis_index("tp"), lax.axis_index("ep")
    y, x = ep // RING, ep % RING
    others = [(tp, y * RING + (x + k) % RING) for k in range(1, RING)]
    z, core, chips, partner, right, left = tp_place()
    greet([partner, right, left] + others)
    depth, quarter = down.shape[0], down.shape[1] // RING
    copies = []
    for k in range(1, RING):
        copy = remote(
            down.at[:, columns((x + k) % RING, quarter)],
            spread.at[pl.ds(k * depth, depth)],
            spread_send.at[k],
            spread_recv.at[k],
            others[k - 1],
        )
        copy.start()
        copies.append(copy)
    keep = pltpu.make_async_copy(down.at[:, columns(x, quarter)], spread.at[pl.ds(0, depth)], spread_send.at[0])
    keep.start()

    def term(block):
        return jnp.dot(context[...], weight[:, columns(block, width)], preferred_element_type=F32)

    total = sum_over_tp(term, total_scratch) + residual[...].astype(F32)
    hidden[:, columns(tp, width)] = total.astype(BF16)
    gather_over_tp(hidden, width, gather_sems)
    keep.wait()
    for copy in copies:
        copy.wait()


def attend(context, weight, residual, down):
    rows, width = residual.shape
    depth, model_width = down.shape
    return pl.pallas_call(
        attend_kernel,
        out_shape=(
            jax.ShapeDtypeStruct((rows, model_width), BF16),
            jax.ShapeDtypeStruct((RING * depth, model_width // RING), BF16),
        ),
        in_specs=in_vmem(3) + [pl.BlockSpec(memory_space=pl.ANY)],
        out_specs=(pl.BlockSpec(memory_space=pltpu.VMEM), pl.BlockSpec(memory_space=pl.ANY)),
        scratch_shapes=sum_scratch(rows, width)
        + [pltpu.SemaphoreType.DMA((4,))] * 4
        + [pltpu.SemaphoreType.DMA((8,))] * 2
        + [pltpu.SemaphoreType.DMA((4,))] * 2,
        compiler_params=pltpu.CompilerParams(
            collective_id=0, has_side_effects=True, vmem_limit_bytes=VMEM_BYTES
        ),
        name="attend",
    )(context, weight, residual, down)


def experts_kernel(packed, gate, up, down, back, rows, gate_up, spread, inner, out, *sems):
    (load, y_send, y_recv, right_send, right_recv, left_send, left_recv,
     far_send, far_recv, in_send, in_recv, out_send, out_recv) = sems
    tp, ep = lax.axis_index("tp"), lax.axis_index("ep")
    y, x = ep // RING, ep % RING
    slots = packed.shape[0] // RING
    width = packed.shape[1]
    block = RING * slots
    hidden_units = gate.shape[1]
    pieces = hidden_units // 128
    quarter = width // RING

    def device(dy, dx):
        return (tp, ((y + dy + RING) % RING) * RING + (x + dx + RING) % RING)

    greet([device(dy, dx) for dy in range(RING) for dx in range(RING) if dy or dx])

    def chunk(r, d):
        return pl.ds(r * block + d * slots, slots)

    y_copies = {}
    for d in (1, 3, 2):
        y_copies[d] = remote(packed.at[chunk(0, d)], rows.at[chunk(0, d)], y_send.at[d], y_recv.at[d], device(d, 0))
        y_copies[d].start()
    right, left = device(0, 1), device(0, -1)
    copies = []

    def to_sides(d, source):
        pair = (
            remote(source, rows.at[chunk(1, d)], right_send.at[d], right_recv.at[d], right),
            remote(source, rows.at[chunk(3, d)], left_send.at[d], left_recv.at[d], left),
        )
        for copy in pair:
            copy.start()
            copies.append(copy)
        return pair

    sides = {0: to_sides(0, packed.at[chunk(0, 0)])}
    loads = []
    for j in range(pieces):
        loads.append((gate.at[:, pl.ds(j * 128, 128)], gate_up.at[:, pl.ds(j * 256, 128)]))
        loads.append((up.at[:, pl.ds(j * 128, 128)], gate_up.at[:, pl.ds(j * 256 + 128, 128)]))
    loads.append((down, spread))
    loads.append((packed.at[chunk(0, 0)], rows.at[chunk(0, 0)]))
    loads = [pltpu.make_async_copy(a, b, load.at[i]) for i, (a, b) in enumerate(loads)]
    for copy in loads:
        copy.start()

    def y_arrived(d):
        y_copies[d].wait_recv()
        sides[d] = to_sides(d, rows.at[chunk(0, d)])

    def unit(r, h):
        span = pl.ds(r * block + h * 2 * slots, 2 * slots)

        def step(j, carry):
            both = jnp.dot(rows[span], gate_up[:, columns(j, 256)], preferred_element_type=F32)
            value, scale = both[:, :128], both[:, 128:]
            inner[span, columns(j, 128)] = (value / (1.0 + jnp.exp(-value)) * scale).astype(BF16)
            return carry

        lax.fori_loop(0, pieces, step, 0)
        for k in range(1, RING):
            there = (r + k) % RING
            copy = remote(
                inner.at[span, pl.ds(0, hidden_units)],
                inner.at[pl.ds(there * block + h * 2 * slots, 2 * slots), pl.ds(k * hidden_units, hidden_units)],
                in_send.at[r, h, k],
                in_recv.at[there, h, k],
                device(0, k),
            )
            copy.start()
            copies.append(copy)

    def came_right(d):
        sides[d][0].wait_recv()

    def came_left(d):
        sides[d][1].wait_recv()

    far = {}

    def onward(d):
        r = 1 if d % 2 == 0 else 3
        far[d] = remote(
            rows.at[chunk(r, d)],
            rows.at[chunk(2, d)],
            far_send.at[d],
            far_recv.at[d],
            right if r == 1 else left,
        )
        far[d].start()
        copies.append(far[d])

    def finish(r, h):
        span = pl.ds(r * block + h * 2 * slots, 2 * slots)
        for k in range(1, RING):
            ref = inner.at[span, pl.ds(k * hidden_units, hidden_units)]
            remote(ref, ref, in_send.at[r, h, k], in_recv.at[r, h, k], device(0, k)).wait_recv()

        def step(n, carry):
            out[span, columns(n, 256)] = jnp.dot(
                inner[span], spread[:, columns(n, 256)], preferred_element_type=F32
            ).astype(BF16)
            return carry

        lax.fori_loop(0, quarter // 256, step, 0)
        for d in (2 * h, 2 * h + 1):
            target = back.at[pl.ds(d * slots, slots), columns(x, quarter)]
            if r == 0 and d == 0:
                copy = pltpu.make_async_copy(out.at[chunk(0, 0)], target, out_send.at[0, 0])
            else:
                copy = remote(out.at[chunk(r, d)], target, out_send.at[r, d], out_recv.at[r, d], device(-d, -r))
            copy.start()
            if r == 0 and d == 0:
                own_back.append(copy)
            else:
                copies.append(copy)

    own_back = []
    y_arrived(1)
    for copy in loads:
        copy.wait()
    unit(0, 0)
    y_arrived(3)
    y_arrived(2)
    unit(0, 1)
    came_right(0)
    onward(0)
    came_left(0)
    came_left(1)
    onward(1)
    came_right(1)
    unit(1, 0)
    unit(3, 0)
    came_left(3)
    onward(3)
    came_right(3)
    came_right(2)
    onward(2)
    came_left(2)
    unit(1, 1)
    unit(3, 1)
    far[0].wait_recv()
    far[1].wait_recv()
    unit(2, 0)
    for r in (0, 1, 3, 2):
        finish(r, 0)
    far[2].wait_recv()
    far[3].wait_recv()
    unit(2, 1)
    for r in (0, 1, 3, 2):
        finish(r, 1)
    own_back[0].wait()
    for r in range(RING):
        for d in range(RING):
            if r or d:
                ref = back.at[pl.ds(d * slots, slots), columns((x + r) % RING, quarter)]
                remote(ref, ref, out_send.at[r, d], out_recv.at[r, d], device(d, r)).wait_recv()
    for copy in y_copies.values():
        copy.wait_send()
    for copy in copies:
        copy.wait_send()


def experts(packed, gate, up, down):
    total, width = packed.shape
    hidden_units = gate.shape[1]
    dma = pltpu.SemaphoreType.DMA
    return pl.pallas_call(
        experts_kernel,
        out_shape=jax.ShapeDtypeStruct((total, width), BF16),
        in_specs=in_vmem(1) + [pl.BlockSpec(memory_space=pl.ANY)] * 3,
        out_specs=pl.BlockSpec(memory_space=pltpu.VMEM),
        scratch_shapes=[
            pltpu.VMEM((RING * total, width), BF16),
            pltpu.VMEM((width, 2 * hidden_units), BF16),
            pltpu.VMEM((RING * hidden_units, width // RING), BF16),
            pltpu.VMEM((RING * total, RING * hidden_units), BF16),
            pltpu.VMEM((RING * total, width // RING), BF16),
            dma((hidden_units // 128 * 2 + 2,)),
        ]
        + [dma((RING,))] * 8
        + [dma((RING, 2, RING))] * 2
        + [dma((RING, RING))] * 2,
        compiler_params=pltpu.CompilerParams(
            collective_id=1, has_side_effects=True, vmem_limit_bytes=VMEM_BYTES
        ),
        name="experts",
    )(packed, gate, up, down)


def mix_kernel(gates, back, state, layer_out, *scratch):
    width = state.shape[1]
    z, core, chips, partner, right, left = tp_place()
    greet([partner, right, left])

    def term(block):
        return jnp.dot(gates[...], back[:, columns(block, width)], preferred_element_type=F32)

    layer_out[...] = (sum_over_tp(term, scratch) + state[...].astype(F32)).astype(BF16)


def mix(gates, back, state):
    rows, width = state.shape
    return pl.pallas_call(
        mix_kernel,
        out_shape=jax.ShapeDtypeStruct((rows, width), BF16),
        in_specs=in_vmem(3),
        out_specs=pl.BlockSpec(memory_space=pltpu.VMEM),
        scratch_shapes=sum_scratch(rows, width),
        compiler_params=pltpu.CompilerParams(
            collective_id=2, has_side_effects=True, vmem_limit_bytes=VMEM_BYTES
        ),
        name="mix",
    )(gates, back, state)


def route(hidden, norm_gain, router_weight, expert_ids, capacity):
    tp, ep = lax.axis_index("tp"), lax.axis_index("ep")
    y = ep // RING
    rows = hidden.shape[0]
    expert_count = router_weight.shape[0]
    state_float = hidden.astype(F32)
    inv_rms = lax.rsqrt(jnp.mean(state_float * state_float, axis=1, keepdims=True) + epsilon)
    normed = (state_float * inv_rms * norm_gain.astype(F32)).astype(BF16)
    logits = lax.dot_general(normed, router_weight, (((1,), (1,)), ((), ())), preferred_element_type=F32)
    every = lax.broadcasted_iota(jnp.int32, (1, 1, expert_count), 2)
    hit_all = jnp.any(expert_ids[:, :, None] == every, axis=1)
    top = jnp.max(jnp.where(hit_all, logits, -jnp.inf), axis=1, keepdims=True)
    raised = jnp.where(hit_all, jnp.exp(jnp.where(hit_all, logits - top, 0.0)), 0.0)
    gates_all = raised / jnp.sum(raised, axis=1, keepdims=True)
    mine = tp * RING + (y + lax.broadcasted_iota(jnp.int32, (1, 1, RING), 2)) % RING
    hit = jnp.any(expert_ids[:, :, None] == mine, axis=1)
    own_gates = jnp.sum(
        jnp.where(lax.broadcasted_iota(jnp.int32, (1, expert_count, 1), 1) == mine, gates_all[:, :, None], 0.0), axis=1
    )
    before = (
        lax.broadcasted_iota(jnp.int32, (rows, rows), 1) <= lax.broadcasted_iota(jnp.int32, (rows, rows), 0)
    ).astype(BF16)
    slot_of = jnp.dot(before, hit.astype(BF16), preferred_element_type=F32).astype(jnp.int32) - 1
    slots = lax.broadcasted_iota(jnp.int32, (1, 1, capacity), 2)
    chosen = (slot_of[:, :, None] == slots) & hit[:, :, None]
    selector = chosen.astype(BF16).reshape(rows, RING * capacity)
    gate_matrix = jnp.where(chosen, own_gates[:, :, None], 0.0).astype(BF16).reshape(rows, RING * capacity)
    packed = lax.dot_general(
        selector, normed, (((0,), (0,)), ((), ())), preferred_element_type=F32
    ).astype(BF16)
    return packed, gate_matrix


def shards(
    context, out_weight, residual, norm_gain, router_weight, expert_ids, w_gate, w_up, w_down
):
    tp = lax.axis_index("tp")
    rows, width = residual.shape
    hidden, spread_down = attend(context, out_weight, residual, w_down[0])
    capacity = min(rows, 2 * rows * expert_ids.shape[1] // router_weight.shape[0])
    packed, gate_matrix = route(hidden, norm_gain, router_weight, expert_ids, capacity)
    back = experts(packed, w_gate[0], w_up[0], spread_down)
    state = lax.dynamic_slice_in_dim(hidden, tp * width, width, 1)
    return mix(gate_matrix, back, state)


def solution(mesh):
    in_specs = (
        P("ep", "tp"),
        P("tp", None),
        P("ep", "tp"),
        P(),
        P(),
        P("ep", None),
        P(("tp", "ep"), None, None),
        P(("tp", "ep"), None, None),
        P(("tp", "ep"), None, None),
    )
    out_specs = P("ep", "tp")
    return jax.shard_map(shards, mesh=mesh, in_specs=in_specs, out_specs=out_specs, check_vma=False)
```

```python
import functools

import jax
import jax.numpy as jnp
from jax import lax
from jax.experimental import pallas as pl
from jax.experimental.pallas import tpu as pltpu
from jax.sharding import PartitionSpec as P

SPLIT = 4
RING = 4
epsilon = 1e-06
MESH = pl.DeviceIdType.MESH
F32 = jnp.float32
BF16 = jnp.bfloat16
VMEM_BYTES = 58 * 2**20
DISTANCES = (4, 3, 5, 2, 6, 1, 7, 0)


def in_vmem(count):
    return [pl.BlockSpec(memory_space=pltpu.VMEM)] * count


def columns(index, width):
    return pl.ds(pl.multiple_of(index * width, width), width)


def greet(devices):
    barrier = pltpu.get_barrier_semaphore()
    for device in devices:
        pl.semaphore_signal(barrier, inc=1, device_id=device, device_id_type=MESH)
    pl.semaphore_wait(barrier, len(devices))


def remote(source, target, send, recv, device):
    return pltpu.make_async_remote_copy(
        src_ref=source, dst_ref=target, send_sem=send, recv_sem=recv, device_id=device, device_id_type=MESH
    )


def tp_place():
    tp, ep = lax.axis_index("tp"), lax.axis_index("ep")
    chips = lax.axis_size("tp") // 2
    z, core = tp // 2, tp % 2
    partner = (z * 2 + 1 - core, ep)
    right = (((z + 1) % chips) * 2 + core, ep)
    left = (((z + chips - 1) % chips) * 2 + core, ep)
    return z, core, chips, partner, right, left


def sum_scratch(rows, width):
    block = (rows, width)
    return [
        pltpu.VMEM((8, *block), BF16),
        pltpu.VMEM((8, *block), BF16),
        pltpu.VMEM((2, 4, *block), BF16),
        pltpu.VMEM((2, 4, *block), BF16),
        pltpu.SemaphoreType.DMA((8,)),
        pltpu.SemaphoreType.DMA((8,)),
        pltpu.SemaphoreType.DMA((2, 4)),
        pltpu.SemaphoreType.DMA((2, 4)),
    ]


def sum_over_tp(term, scratch):
    swap_out, swap_in, arm_out, arm_in, swap_send, swap_recv, arm_send, arm_recv = scratch
    z, core, chips, partner, right, left = tp_place()
    half = swap_out.shape[1] // 2
    whole = pl.ds(0, 2 * half)
    parts = (pl.ds(0, half), pl.ds(half, half))
    swaps = []
    for j in DISTANCES:
        block = ((z + j) % chips) * 2 + 1 - core
        swap_out[j] = term(block).astype(BF16)
        copy = remote(swap_out.at[j], swap_in.at[j], swap_send.at[j], swap_recv.at[j], partner)
        copy.start()
        swaps.append(copy)
    swaps = dict(zip(DISTANCES, swaps))

    def pair(j):
        mine = term(((z + j) % chips) * 2 + core)
        swaps[j].wait_recv()
        return mine + swap_in[j].astype(F32)

    sent = []

    def pass_on(arm, step, span):
        copy = remote(
            arm_out.at[arm, step, span],
            arm_in.at[arm, step, span],
            arm_send.at[arm, step],
            arm_recv.at[arm, step],
            (right, left)[arm],
        )
        copy.start()
        sent.append(copy)
        return copy

    far = pair(4)
    last = [None, None]
    for arm in range(2):
        arm_out[arm, 0, parts[arm]] = far[arm * half : (arm + 1) * half].astype(BF16)
        last[arm] = pass_on(arm, 0, parts[arm])
    for step in range(1, 4):
        for arm in range(2):
            mine = pair(4 - step if arm == 0 else 4 + step)
            last[arm].wait_recv()
            if step == 1:
                arm_out[arm, step] = mine.astype(BF16)
                span = parts[arm]
                came = arm_in[arm, 0, span].astype(F32)
                arm_out[arm, step, span] = (mine[arm * half : (arm + 1) * half] + came).astype(BF16)
            else:
                arm_out[arm, step] = (mine + arm_in[arm, step - 1].astype(F32)).astype(BF16)
            last[arm] = pass_on(arm, step, whole)
    total = pair(0)
    for arm in range(2):
        last[arm].wait_recv()
        total = total + arm_in[arm, 3].astype(F32)
    for copy in sent:
        copy.wait_send()
    for j in DISTANCES:
        swaps[j].wait_send()
    return total


def gather_over_tp(out, width, sems):
    right_send, right_recv, left_send, left_recv, near_send, near_recv = sems
    z, core, chips, partner, right, left = tp_place()
    half = out.shape[0] // 2
    whole = pl.ds(0, 2 * half)
    parts = (pl.ds(0, half), pl.ds(half, half))

    def at(j, span, side):
        return out.at[span, columns(((z + j + chips) % chips) * 2 + side, width)]

    copies = []

    def go(j, span, send, recv, device):
        ref = at(j, span, core)
        copy = remote(ref, ref, send, recv, device)
        copy.start()
        copies.append(copy)

    go(0, whole, right_send.at[0], right_recv.at[0], right)
    go(0, whole, left_send.at[0], left_recv.at[0], left)
    go(0, whole, near_send.at[0], near_recv.at[0], partner)
    for step in range(1, 5):
        span_r = parts[0] if step == 4 else whole
        span_l = parts[1] if step == 4 else whole
        ref = at(-step, span_r, core)
        remote(ref, ref, right_send.at[step - 1], right_recv.at[step - 1], right).wait_recv()
        if step < 4:
            go(-step, parts[0] if step == 3 else whole, right_send.at[step], right_recv.at[step], right)
            go(-step, whole, near_send.at[step], near_recv.at[step], partner)
        ref = at(step, span_l, core)
        remote(ref, ref, left_send.at[step - 1], left_recv.at[step - 1], left).wait_recv()
        if step < 4:
            go(step, parts[1] if step == 3 else whole, left_send.at[step], left_recv.at[step], left)
            go(step, whole, near_send.at[8 - step], near_recv.at[8 - step], partner)
    go(4, whole, near_send.at[4], near_recv.at[4], partner)
    for j in range(8):
        ref = at(-j, whole, 1 - core)
        remote(ref, ref, near_send.at[j], near_recv.at[j], partner).wait_recv()
    for copy in copies:
        copy.wait_send()


def attend_kernel(context, weight, residual, down, hidden, spread, *scratch):
    total_scratch, gather_sems, (spread_send, spread_recv) = scratch[:8], scratch[8:14], scratch[14:16]
    width = residual.shape[1]
    tp, ep = lax.axis_index("tp"), lax.axis_index("ep")
    y, x = ep // RING, ep % RING
    others = [(tp, y * RING + (x + k) % RING) for k in range(1, RING)]
    z, core, chips, partner, right, left = tp_place()
    greet([partner, right, left] + others)
    depth, quarter = down.shape[0], down.shape[1] // RING
    copies = []
    for k in range(1, RING):
        copy = remote(
            down.at[:, columns((x + k) % RING, quarter)],
            spread.at[pl.ds(k * depth, depth)],
            spread_send.at[k],
            spread_recv.at[k],
            others[k - 1],
        )
        copy.start()
        copies.append(copy)
    keep = pltpu.make_async_copy(down.at[:, columns(x, quarter)], spread.at[pl.ds(0, depth)], spread_send.at[0])
    keep.start()

    def term(block):
        return jnp.dot(context[...], weight[:, columns(block, width)], preferred_element_type=F32)

    total = sum_over_tp(term, total_scratch) + residual[...].astype(F32)
    hidden[:, columns(tp, width)] = total.astype(BF16)
    gather_over_tp(hidden, width, gather_sems)
    keep.wait()
    for copy in copies:
        copy.wait()


def attend(context, weight, residual, down):
    rows, width = residual.shape
    depth, model_width = down.shape
    return pl.pallas_call(
        attend_kernel,
        out_shape=(
            jax.ShapeDtypeStruct((rows, model_width), BF16),
            jax.ShapeDtypeStruct((RING * depth, model_width // RING), BF16),
        ),
        in_specs=in_vmem(3) + [pl.BlockSpec(memory_space=pl.ANY)],
        out_specs=(pl.BlockSpec(memory_space=pltpu.VMEM), pl.BlockSpec(memory_space=pl.ANY)),
        scratch_shapes=sum_scratch(rows, width)
        + [pltpu.SemaphoreType.DMA((4,))] * 4
        + [pltpu.SemaphoreType.DMA((8,))] * 2
        + [pltpu.SemaphoreType.DMA((4,))] * 2,
        compiler_params=pltpu.CompilerParams(
            collective_id=0, has_side_effects=True, vmem_limit_bytes=VMEM_BYTES
        ),
        name="attend",
    )(context, weight, residual, down)


def experts_kernel(packed, meta, gate, up, down, back, meta_all, rows, gate_up, spread, inner, out, *sems):
    (load, y_send, y_recv, right_send, right_recv, left_send, left_recv, far_send, far_recv, meta_send, meta_recv,
     in_send, in_recv, on_send, on_recv, out_send, out_recv) = sems
    tp, ep = lax.axis_index("tp"), lax.axis_index("ep")
    y, x = ep // RING, ep % RING
    slots = packed.shape[0] // RING
    width = packed.shape[1]
    block = RING * slots
    hidden_units = gate.shape[1]
    pieces = hidden_units // 128
    quarter = width // RING

    def device(dy, dx):
        return (tp, ((y + dy + RING) % RING) * RING + (x + dx + RING) % RING)

    right, left = device(0, 1), device(0, -1)
    greet([device(0, k) for k in range(1, RING)] + [device(k, 0) for k in range(1, RING)])

    def chunk(r, d):
        return pl.ds(r * block + d * slots, slots)

    def unit_span(r, h):
        return pl.ds(r * block + h * 2 * slots, 2 * slots)

    def inner_columns(k):
        return pl.ds(k * hidden_units, hidden_units)

    copies = []

    def send(source, target, send_sem, recv_sem, to):
        copy = remote(source, target, send_sem, recv_sem, to)
        copy.start()
        copies.append(copy)
        return copy

    y_copies = {}
    for d in (1, 3, 2):
        y_copies[d] = send(packed.at[chunk(0, d)], rows.at[chunk(0, d)], y_send.at[d], y_recv.at[d], device(d, 0))

    def to_sides(d, source):
        return (
            send(source, rows.at[chunk(1, d)], right_send.at[d], right_recv.at[d], right),
            send(source, rows.at[chunk(3, d)], left_send.at[d], left_recv.at[d], left),
        )

    sides = {0: to_sides(0, packed.at[chunk(0, 0)])}
    loads = []
    for j in range(pieces):
        loads.append((gate.at[:, pl.ds(j * 128, 128)], gate_up.at[:, pl.ds(j * 256, 128)]))
        loads.append((up.at[:, pl.ds(j * 128, 128)], gate_up.at[:, pl.ds(j * 256 + 128, 128)]))
    loads.append((down, spread))
    loads.append((packed.at[chunk(0, 0)], rows.at[chunk(0, 0)]))
    loads.append((meta, meta_all.at[pl.ds(0, 2 * RING)]))
    loads = [pltpu.make_async_copy(a, b, load.at[i]) for i, (a, b) in enumerate(loads)]
    for copy in loads:
        copy.start()
    metas = [
        send(meta, meta_all.at[pl.ds(k * 2 * RING, 2 * RING)], meta_send.at[k], meta_recv.at[k], device(0, k))
        for k in range(1, RING)
    ]

    def y_arrived(d):
        y_copies[d].wait_recv()
        sides[d] = to_sides(d, rows.at[chunk(0, d)])

    def unit(r, h):
        span = unit_span(r, h)

        def step(j, carry):
            both = jnp.dot(rows[span], gate_up[:, columns(j, 256)], preferred_element_type=F32)
            value, scale = both[:, :128], both[:, 128:]
            inner[span, columns(j, 128)] = (value / (1.0 + jnp.exp(-value)) * scale).astype(BF16)
            return carry

        lax.fori_loop(0, pieces, step, 0)
        for k in (1, 3):
            there = (r + k) % RING
            send(
                inner.at[span, inner_columns(0)],
                inner.at[unit_span(there, h), inner_columns(k)],
                in_send.at[r, h, k],
                in_recv.at[there, h, k],
                device(0, k),
            )

    def relay(r, h):
        for side, k in ((0, 1), (1, 3)):
            here, there = (r + k) % RING, (r + 2) % RING
            ref = inner.at[unit_span(here, h), inner_columns(k)]
            remote(ref, ref, in_send.at[r, h, k], in_recv.at[here, h, k], right).wait_recv()
            send(
                inner.at[chunk(here, 2 * h + side), inner_columns(k)],
                inner.at[chunk(there, 2 * h + side), inner_columns(2)],
                on_send.at[r, h, side],
                on_recv.at[there, h, side],
                (right, left)[side],
            )

    def came_right(d):
        sides[d][0].wait_recv()

    def came_left(d):
        sides[d][1].wait_recv()

    far = {}

    def onward(d):
        r = 1 if d % 2 == 0 else 3
        far[d] = send(
            rows.at[chunk(r, d)], rows.at[chunk(2, d)], far_send.at[d], far_recv.at[d], right if r == 1 else left
        )

    def finish(r, h):
        span = unit_span(r, h)
        for side in range(2):
            ref = inner.at[chunk(r, 2 * h + side), inner_columns(2)]
            remote(ref, ref, on_send.at[r, h, side], on_recv.at[r, h, side], right).wait_recv()

        def step(n, carry):
            out[span, columns(n, 256)] = jnp.dot(
                inner[span], spread[:, columns(n, 256)], preferred_element_type=F32
            ).astype(BF16)
            return carry

        lax.fori_loop(0, quarter // 256, step, 0)
        for d in (2 * h, 2 * h + 1):
            target = back.at[chunk(r, d)]
            if d == 0:
                copy = pltpu.make_async_copy(out.at[chunk(r, 0)], target, out_send.at[r, 0])
                copy.start()
                kept.append(copy)
            else:
                send(out.at[chunk(r, d)], target, out_send.at[r, d], out_recv.at[r, d], device(-d, 0))

    kept = []
    y_arrived(1)
    for copy in loads:
        copy.wait()
    unit(0, 0)
    y_arrived(3)
    y_arrived(2)
    came_right(0)
    onward(0)
    came_left(0)
    came_left(1)
    onward(1)
    came_right(1)
    unit(1, 0)
    unit(3, 0)
    relay(0, 0)
    unit(0, 1)
    relay(1, 0)
    relay(3, 0)
    far[0].wait_recv()
    far[1].wait_recv()
    unit(2, 0)
    came_left(3)
    onward(3)
    came_right(3)
    came_right(2)
    onward(2)
    came_left(2)
    unit(1, 1)
    unit(3, 1)
    relay(2, 0)
    relay(0, 1)
    relay(1, 1)
    relay(3, 1)
    for r in (0, 1, 3, 2):
        finish(r, 0)
    far[2].wait_recv()
    far[3].wait_recv()
    unit(2, 1)
    relay(2, 1)
    for r in (0, 1, 3, 2):
        finish(r, 1)
    for copy in kept:
        copy.wait()
    for r in range(RING):
        for d in range(1, RING):
            ref = back.at[chunk(r, d)]
            remote(ref, ref, out_send.at[r, d], out_recv.at[r, d], device(d, 0)).wait_recv()
    for copy in metas:
        copy.wait_recv()
    for copy in copies:
        copy.wait_send()


def experts(packed, meta, gate, up, down):
    total, width = packed.shape
    hidden_units = gate.shape[1]
    dma = pltpu.SemaphoreType.DMA
    return pl.pallas_call(
        experts_kernel,
        out_shape=(
            jax.ShapeDtypeStruct((RING * total, width // RING), BF16),
            jax.ShapeDtypeStruct((RING * meta.shape[0], meta.shape[1]), F32),
        ),
        in_specs=in_vmem(2) + [pl.BlockSpec(memory_space=pl.ANY)] * 3,
        out_specs=tuple(in_vmem(2)),
        scratch_shapes=[
            pltpu.VMEM((RING * total, width), BF16),
            pltpu.VMEM((width, 2 * hidden_units), BF16),
            pltpu.VMEM((RING * hidden_units, width // RING), BF16),
            pltpu.VMEM((RING * total, RING * hidden_units), BF16),
            pltpu.VMEM((RING * total, width // RING), BF16),
            dma((hidden_units // 128 * 2 + 3,)),
        ]
        + [dma((RING,))] * 10
        + [dma((RING, 2, RING))] * 2
        + [dma((RING, 2, 2))] * 2
        + [dma((RING, RING))] * 2,
        compiler_params=pltpu.CompilerParams(
            collective_id=1, has_side_effects=True, vmem_limit_bytes=VMEM_BYTES
        ),
        name="experts",
    )(packed, meta, gate, up, down)


def mix_kernel(meta, back, state, layer_out, share_out, share_in, matrix, share_send, share_recv, *scratch):
    rows, width = state.shape
    slots = back.shape[0] // RING // RING
    tp, ep = lax.axis_index("tp"), lax.axis_index("ep")
    y, x = ep // RING, ep % RING
    z, core, chips, partner, right, left = tp_place()

    def group_of(block):
        return (block // RING - x + 2 + RING) % RING

    target = (x * RING + tp % RING, y * RING + (x - group_of(tp) + RING) % RING)
    from_x = tp // RING
    shift = (from_x - x + RING) % RING
    source = (((from_x + shift + 2) % RING) * RING + tp % RING, y * RING + from_x)
    greet([partner, right, left, target, source])
    place = lax.broadcasted_iota(jnp.int32, (slots, rows), 0).astype(F32)
    for r in range(RING):
        for d in range(RING):
            slot = meta[pl.ds(r * 2 * RING + d, 1)]
            gate = meta[pl.ds(r * 2 * RING + RING + d, 1)]
            matrix[pl.ds((r * RING + d) * slots, slots)] = jnp.where(slot == place, gate, 0.0).astype(BF16)

    def term(block):
        span = pl.ds(pl.multiple_of(group_of(block) * RING * slots, RING * slots), RING * slots)
        return lax.dot_general(
            matrix[span],
            back[span, columns(block % RING, width)],
            (((0,), (0,)), ((), ())),
            preferred_element_type=F32,
        )

    share_out[...] = sum_over_tp(term, scratch).astype(BF16)
    copy = remote(share_out, share_in, share_send.at[0], share_recv.at[0], target)
    copy.start()
    copy.wait()
    layer_out[...] = (share_in[...].astype(F32) + state[...].astype(F32)).astype(BF16)


def mix(meta, back, state):
    rows, width = state.shape
    return pl.pallas_call(
        mix_kernel,
        out_shape=jax.ShapeDtypeStruct((rows, width), BF16),
        in_specs=in_vmem(3),
        out_specs=pl.BlockSpec(memory_space=pltpu.VMEM),
        scratch_shapes=[
            pltpu.VMEM((rows, width), BF16),
            pltpu.VMEM((rows, width), BF16),
            pltpu.VMEM((back.shape[0], rows), BF16),
            pltpu.SemaphoreType.DMA((1,)),
            pltpu.SemaphoreType.DMA((1,)),
        ]
        + sum_scratch(rows, width),
        compiler_params=pltpu.CompilerParams(
            collective_id=2, has_side_effects=True, vmem_limit_bytes=VMEM_BYTES
        ),
        name="mix",
    )(meta, back, state)


def route(hidden, norm_gain, router_weight, expert_ids, capacity):
    tp, ep = lax.axis_index("tp"), lax.axis_index("ep")
    y = ep // RING
    rows = hidden.shape[0]
    expert_count = router_weight.shape[0]
    state_float = hidden.astype(F32)
    inv_rms = lax.rsqrt(jnp.mean(state_float * state_float, axis=1, keepdims=True) + epsilon)
    normed = (state_float * inv_rms * norm_gain.astype(F32)).astype(BF16)
    logits = lax.dot_general(normed, router_weight, (((1,), (1,)), ((), ())), preferred_element_type=F32)
    every = lax.broadcasted_iota(jnp.int32, (1, 1, expert_count), 2)
    hit_all = jnp.any(expert_ids[:, :, None] == every, axis=1)
    top = jnp.max(jnp.where(hit_all, logits, -jnp.inf), axis=1, keepdims=True)
    raised = jnp.where(hit_all, jnp.exp(jnp.where(hit_all, logits - top, 0.0)), 0.0)
    gates_all = raised / jnp.sum(raised, axis=1, keepdims=True)
    mine = tp * RING + (y + lax.broadcasted_iota(jnp.int32, (1, 1, RING), 2)) % RING
    hit = jnp.any(expert_ids[:, :, None] == mine, axis=1)
    own_gates = jnp.sum(
        jnp.where(lax.broadcasted_iota(jnp.int32, (1, expert_count, 1), 1) == mine, gates_all[:, :, None], 0.0), axis=1
    )
    before = (
        lax.broadcasted_iota(jnp.int32, (rows, rows), 1) <= lax.broadcasted_iota(jnp.int32, (rows, rows), 0)
    ).astype(BF16)
    slot_of = jnp.dot(before, hit.astype(BF16), preferred_element_type=F32).astype(jnp.int32) - 1
    slots = lax.broadcasted_iota(jnp.int32, (1, 1, capacity), 2)
    chosen = (slot_of[:, :, None] == slots) & hit[:, :, None]
    selector = chosen.astype(BF16).reshape(rows, RING * capacity)
    places = jnp.where(hit, slot_of, -1).astype(F32)
    meta = jnp.concatenate([places, own_gates], axis=1).T
    packed = lax.dot_general(
        selector, normed, (((0,), (0,)), ((), ())), preferred_element_type=F32
    ).astype(BF16)
    return packed, meta


def shards(
    context, out_weight, residual, norm_gain, router_weight, expert_ids, w_gate, w_up, w_down
):
    tp = lax.axis_index("tp")
    rows, width = residual.shape
    hidden, spread_down = attend(context, out_weight, residual, w_down[0])
    capacity = min(rows, 2 * rows * expert_ids.shape[1] // router_weight.shape[0])
    packed, meta = route(hidden, norm_gain, router_weight, expert_ids, capacity)
    back, meta_all = experts(packed, meta, w_gate[0], w_up[0], spread_down)
    state = lax.dynamic_slice_in_dim(hidden, tp * width, width, 1)
    return mix(meta_all, back, state)


def solution(mesh):
    in_specs = (
        P("ep", "tp"),
        P("tp", None),
        P("ep", "tp"),
        P(),
        P(),
        P("ep", None),
        P(("tp", "ep"), None, None),
        P(("tp", "ep"), None, None),
        P(("tp", "ep"), None, None),
    )
    out_specs = P("ep", "tp")
    return jax.shard_map(shards, mesh=mesh, in_specs=in_specs, out_specs=out_specs, check_vma=False)
```

```python
import functools

import jax
import jax.numpy as jnp
from jax import lax
from jax.experimental import pallas as pl
from jax.experimental.pallas import tpu as pltpu
from jax.sharding import PartitionSpec as P

SPLIT = 4
RING = 4
epsilon = 1e-06
MESH = pl.DeviceIdType.MESH
F32 = jnp.float32
BF16 = jnp.bfloat16
VMEM_BYTES = 58 * 2**20
PLACE = (3, 0, 2, 1)
STAGES = ((1, 3), (2,), (0,))
DISTANCES = (4, 3, 5, 2, 6, 1, 7, 0)


def in_vmem(count):
    return [pl.BlockSpec(memory_space=pltpu.VMEM)] * count


def columns(index, width):
    return pl.ds(pl.multiple_of(index * width, width), width)


def greet(devices):
    barrier = pltpu.get_barrier_semaphore()
    for device in devices:
        pl.semaphore_signal(barrier, inc=1, device_id=device, device_id_type=MESH)
    pl.semaphore_wait(barrier, len(devices))


def remote(source, target, send, recv, device):
    return pltpu.make_async_remote_copy(
        src_ref=source, dst_ref=target, send_sem=send, recv_sem=recv, device_id=device, device_id_type=MESH
    )


def tp_place():
    tp, ep = lax.axis_index("tp"), lax.axis_index("ep")
    chips = lax.axis_size("tp") // 2
    z, core = tp // 2, tp % 2
    partner = (z * 2 + 1 - core, ep)
    right = (((z + 1) % chips) * 2 + core, ep)
    left = (((z + chips - 1) % chips) * 2 + core, ep)
    return z, core, chips, partner, right, left


def sum_scratch(rows, width):
    block = (rows, width)
    return [
        pltpu.VMEM((8, *block), BF16),
        pltpu.VMEM((8, *block), BF16),
        pltpu.VMEM((8, *block), F32),
        pltpu.VMEM((2, 4, *block), BF16),
        pltpu.VMEM((2, 4, *block), BF16),
        pltpu.SemaphoreType.DMA((8,)),
        pltpu.SemaphoreType.DMA((8,)),
        pltpu.SemaphoreType.DMA((2, 4, 2)),
        pltpu.SemaphoreType.DMA((2, 4, 2)),
    ]


def sum_over_tp(term, give, scratch):
    swap_out, swap_in, pairs, arm_out, arm_in, swap_send, swap_recv, arm_send, arm_recv = scratch
    z, core, chips, partner, right, left = tp_place()
    half = swap_out.shape[1] // 2
    spans = (pl.ds(0, half), pl.ds(half, half))
    swaps = {}
    for j in DISTANCES:
        swap_out[j] = term(((z + j) % chips) * 2 + 1 - core).astype(BF16)
        swaps[j] = remote(swap_out.at[j], swap_in.at[j], swap_send.at[j], swap_recv.at[j], partner)
        swaps[j].start()

    def pair(j):
        mine = term(((z + j) % chips) * 2 + core)
        swaps[j].wait_recv()
        pairs[j] = mine + swap_in[j].astype(F32)

    hops = {}

    def hop(arm, h, step):
        value = pairs[4 - step if arm == 0 else 4 + step, spans[h]]
        if (arm, h, step - 1) in hops:
            hops[arm, h, step - 1].wait_recv()
            value = value + arm_in[arm, step - 1, spans[h]].astype(F32)
        arm_out[arm, step, spans[h]] = value.astype(BF16)
        copy = remote(
            arm_out.at[arm, step, spans[h]],
            arm_in.at[arm, step, spans[h]],
            arm_send.at[arm, step, h],
            arm_recv.at[arm, step, h],
            (right, left)[arm],
        )
        copy.start()
        hops[arm, h, step] = copy

    pair(4)
    hop(0, 0, 0)
    hop(1, 1, 0)
    for step in range(1, 4):
        pair(4 - step)
        pair(4 + step)
        hop(0, 1, step)
        hop(1, 0, step)
        hop(0, 0, step)
        hop(1, 1, step)
    pair(0)
    for h in range(2):
        total = pairs[0, spans[h]]
        for arm in (1 - h, h):
            hops[arm, h, 3].wait_recv()
            total = total + arm_in[arm, 3, spans[h]].astype(F32)
        give(h, spans[h], total)
    for copy in list(hops.values()) + list(swaps.values()):
        copy.wait_send()


def gather_over_tp(out, width, sems):
    arm_send, arm_recv, near_send, near_recv = sems
    z, core, chips, partner, right, left = tp_place()
    half = out.shape[0] // 2
    copies = []

    def at(j, h, side):
        return out.at[pl.ds(h * half, half), columns(((z + j + chips) % chips) * 2 + side, width)]

    def pass_on(arm, h, step):
        ref = at(step if arm else -step, h, core)
        copies.append(remote(ref, ref, arm_send.at[arm, step, h], arm_recv.at[arm, step, h], (right, left)[arm]))
        copies[-1].start()

    def to_partner(j, h):
        ref = at(j, h, core)
        copies.append(remote(ref, ref, near_send.at[j % 8, h], near_recv.at[j % 8, h], partner))
        copies[-1].start()

    def start(h):
        for arm in (h, 1 - h):
            pass_on(arm, h, 0)
        to_partner(0, h)

    def finish():
        for step in range(1, 5):
            for arm, h in ((0, 0), (1, 0), (1, 1), (0, 1)):
                if step == 4 and arm != h:
                    continue
                j = step if arm else -step
                ref = at(j, h, core)
                remote(ref, ref, arm_send.at[arm, step - 1, h], arm_recv.at[arm, step - 1, h], right).wait_recv()
                if step < 3 or (step == 3 and arm == h):
                    pass_on(arm, h, step)
                to_partner(j, h)
        for j in range(8):
            for h in range(2):
                ref = at(j, h, 1 - core)
                remote(ref, ref, near_send.at[j, h], near_recv.at[j, h], partner).wait_recv()
        for copy in copies:
            copy.wait_send()

    return start, finish


def attend_kernel(context, weight, residual, down, hidden, spread, *scratch):
    total_scratch, gather_sems, (spread_send, spread_recv) = scratch[:9], scratch[9:13], scratch[13:15]
    width = residual.shape[1]
    tp, ep = lax.axis_index("tp"), lax.axis_index("ep")
    y, x = ep // RING, ep % RING
    others = [(tp, y * RING + (x + k) % RING) for k in range(1, RING)]
    z, core, chips, partner, right, left = tp_place()
    greet([partner, right, left] + others)
    depth, quarter = down.shape[0], down.shape[1] // RING
    copies = []
    for k in range(1, RING):
        copy = remote(
            down.at[:, columns((x + k) % RING, quarter)],
            spread.at[pl.ds(k * depth, depth)],
            spread_send.at[k],
            spread_recv.at[k],
            others[k - 1],
        )
        copy.start()
        copies.append(copy)
    keep = pltpu.make_async_copy(down.at[:, columns(x, quarter)], spread.at[pl.ds(0, depth)], spread_send.at[0])
    keep.start()

    def term(block):
        return jnp.dot(context[...], weight[:, columns(block, width)], preferred_element_type=F32)

    start, finish = gather_over_tp(hidden, width, gather_sems)

    def give(h, span, total):
        hidden[span, columns(tp, width)] = (total + residual[span].astype(F32)).astype(BF16)
        start(h)

    sum_over_tp(term, give, total_scratch)
    finish()
    keep.wait()
    for copy in copies:
        copy.wait()


def attend(context, weight, residual, down):
    rows, width = residual.shape
    depth, model_width = down.shape
    return pl.pallas_call(
        attend_kernel,
        out_shape=(
            jax.ShapeDtypeStruct((rows, model_width), BF16),
            jax.ShapeDtypeStruct((RING * depth, model_width // RING), BF16),
        ),
        in_specs=in_vmem(3) + [pl.BlockSpec(memory_space=pl.ANY)],
        out_specs=(pl.BlockSpec(memory_space=pltpu.VMEM), pl.BlockSpec(memory_space=pl.ANY)),
        scratch_shapes=sum_scratch(rows, width)
        + [pltpu.SemaphoreType.DMA((2, 4, 2))] * 2
        + [pltpu.SemaphoreType.DMA((8, 2))] * 2
        + [pltpu.SemaphoreType.DMA((4,))] * 2,
        compiler_params=pltpu.CompilerParams(
            collective_id=0, has_side_effects=True, vmem_limit_bytes=VMEM_BYTES
        ),
        name="attend",
    )(context, weight, residual, down)


def experts_kernel(packed, meta, gate, up, down, back, meta_all, rows, gate_up, spread, inner, out, *sems):
    (load, y_send, y_recv, right_send, right_recv, left_send, left_recv, far_send, far_recv, meta_send, meta_recv,
     in_send, in_recv, on_send, on_recv, out_send, out_recv) = sems
    tp, ep = lax.axis_index("tp"), lax.axis_index("ep")
    y, x = ep // RING, ep % RING
    slots = packed.shape[0] // RING
    width = packed.shape[1]
    block = RING * slots
    hidden_units = gate.shape[1]
    pieces = hidden_units // 128
    quarter = width // RING

    def device(dy, dx):
        return (tp, ((y + dy + RING) % RING) * RING + (x + dx + RING) % RING)

    right, left = device(0, 1), device(0, -1)
    greet([device(0, k) for k in range(1, RING)] + [device(k, 0) for k in range(1, RING)])

    def chunk(r, d):
        return pl.ds(r * block + PLACE[d] * slots, slots)

    def unit_span(r, h):
        return pl.ds(r * block + PLACE[STAGES[h][0]] * slots, len(STAGES[h]) * slots)

    def half_span(r, h, side):
        half = len(STAGES[h]) * slots // 2
        return pl.ds(r * block + PLACE[STAGES[h][0]] * slots + side * half, half)

    def inner_columns(k):
        return pl.ds(k * hidden_units, hidden_units)

    copies = []

    def send(source, target, send_sem, recv_sem, to):
        copy = remote(source, target, send_sem, recv_sem, to)
        copy.start()
        copies.append(copy)
        return copy

    y_copies = {}
    for d in (1, 3, 2):
        y_copies[d] = send(packed.at[pl.ds(d * slots, slots)], rows.at[chunk(0, d)], y_send.at[d], y_recv.at[d], device(d, 0))

    def to_sides(d, source):
        return (
            send(source, rows.at[chunk(1, d)], right_send.at[d], right_recv.at[d], right),
            send(source, rows.at[chunk(3, d)], left_send.at[d], left_recv.at[d], left),
        )

    sides = {0: to_sides(0, packed.at[pl.ds(0, slots)])}
    loads = []
    for j in range(pieces):
        loads.append((gate.at[:, pl.ds(j * 128, 128)], gate_up.at[:, pl.ds(j * 256, 128)]))
        loads.append((up.at[:, pl.ds(j * 128, 128)], gate_up.at[:, pl.ds(j * 256 + 128, 128)]))
    loads.append((down, spread))
    loads.append((packed.at[pl.ds(0, slots)], rows.at[chunk(0, 0)]))
    loads.append((meta, meta_all.at[pl.ds(0, 2 * RING)]))
    loads = [pltpu.make_async_copy(a, b, load.at[i]) for i, (a, b) in enumerate(loads)]
    for copy in loads:
        copy.start()
    metas = [
        send(meta, meta_all.at[pl.ds(k * 2 * RING, 2 * RING)], meta_send.at[k], meta_recv.at[k], device(0, k))
        for k in range(1, RING)
    ]

    def y_arrived(d):
        y_copies[d].wait_recv()
        sides[d] = to_sides(d, rows.at[chunk(0, d)])

    def unit(r, h):
        span = unit_span(r, h)

        def step(j, carry):
            both = jnp.dot(rows[span], gate_up[:, columns(j, 256)], preferred_element_type=F32)
            value, scale = both[:, :128], both[:, 128:]
            inner[span, columns(j, 128)] = (value / (1.0 + jnp.exp(-value)) * scale).astype(BF16)
            return carry

        lax.fori_loop(0, pieces, step, 0)
        for k in (1, 3):
            there = (r + k) % RING
            send(
                inner.at[span, inner_columns(0)],
                inner.at[unit_span(there, h), inner_columns(k)],
                in_send.at[r, h, k],
                in_recv.at[there, h, k],
                device(0, k),
            )

    def relay(r, h):
        for side, k in ((0, 1), (1, 3)):
            here, there = (r + k) % RING, (r + 2) % RING
            ref = inner.at[unit_span(here, h), inner_columns(k)]
            remote(ref, ref, in_send.at[r, h, k], in_recv.at[here, h, k], right).wait_recv()
            send(
                inner.at[half_span(here, h, side), inner_columns(k)],
                inner.at[half_span(there, h, side), inner_columns(2)],
                on_send.at[r, h, side],
                on_recv.at[there, h, side],
                (right, left)[side],
            )

    def came_right(d):
        sides[d][0].wait_recv()

    def came_left(d):
        sides[d][1].wait_recv()

    far = {}

    def onward(h, side):
        far[h, side] = send(
            rows.at[half_span((1, 3)[side], h, side)],
            rows.at[half_span(2, h, side)],
            far_send.at[h, side],
            far_recv.at[h, side],
            (right, left)[side],
        )

    def came_far(h):
        far[h, 0].wait_recv()
        far[h, 1].wait_recv()

    def finish(r, h):
        span = unit_span(r, h)
        for side in range(2):
            ref = inner.at[half_span(r, h, side), inner_columns(2)]
            remote(ref, ref, on_send.at[r, h, side], on_recv.at[r, h, side], right).wait_recv()

        def step(n, carry):
            out[span, columns(n, 256)] = jnp.dot(
                inner[span], spread[:, columns(n, 256)], preferred_element_type=F32
            ).astype(BF16)
            return carry

        lax.fori_loop(0, quarter // 256, step, 0)
        for d in STAGES[h]:
            target = back.at[chunk(r, d)]
            if d == 0:
                copy = pltpu.make_async_copy(out.at[chunk(r, 0)], target, out_send.at[r, 0])
                copy.start()
                kept.append(copy)
            else:
                send(out.at[chunk(r, d)], target, out_send.at[r, d], out_recv.at[r, d], device(-d, 0))

    kept = []
    y_arrived(1)
    y_arrived(3)
    for copy in loads:
        copy.wait()
    unit(0, 0)
    came_right(0)
    came_left(0)
    unit(0, 2)
    y_arrived(2)
    came_right(1)
    onward(0, 0)
    came_left(3)
    onward(0, 1)
    came_left(1)
    came_right(3)
    unit(1, 0)
    unit(3, 0)
    relay(0, 0)
    unit(1, 2)
    unit(3, 2)
    unit(0, 1)
    came_right(2)
    onward(1, 0)
    came_left(2)
    onward(1, 1)
    relay(1, 0)
    relay(3, 0)
    came_far(0)
    unit(2, 0)
    onward(2, 0)
    onward(2, 1)
    unit(1, 1)
    unit(3, 1)
    relay(0, 1)
    relay(0, 2)
    relay(2, 0)
    for r in (0, 1, 3, 2):
        finish(r, 0)
    relay(1, 1)
    relay(3, 1)
    came_far(1)
    unit(2, 1)
    relay(1, 2)
    relay(3, 2)
    came_far(2)
    unit(2, 2)
    relay(2, 1)
    for r in (0, 1, 3, 2):
        finish(r, 1)
    relay(2, 2)
    for r in (0, 1, 3, 2):
        finish(r, 2)
    for copy in kept:
        copy.wait()
    for r in range(RING):
        for d in range(1, RING):
            ref = back.at[chunk(r, d)]
            remote(ref, ref, out_send.at[r, d], out_recv.at[r, d], device(d, 0)).wait_recv()
    for copy in metas:
        copy.wait_recv()
    for copy in copies:
        copy.wait_send()


def experts(packed, meta, gate, up, down):
    total, width = packed.shape
    hidden_units = gate.shape[1]
    dma = pltpu.SemaphoreType.DMA
    return pl.pallas_call(
        experts_kernel,
        out_shape=(
            jax.ShapeDtypeStruct((RING * total, width // RING), BF16),
            jax.ShapeDtypeStruct((RING * meta.shape[0], meta.shape[1]), F32),
        ),
        in_specs=in_vmem(2) + [pl.BlockSpec(memory_space=pl.ANY)] * 3,
        out_specs=tuple(in_vmem(2)),
        scratch_shapes=[
            pltpu.VMEM((RING * total, width), BF16),
            pltpu.VMEM((width, 2 * hidden_units), BF16),
            pltpu.VMEM((RING * hidden_units, width // RING), BF16),
            pltpu.VMEM((RING * total, RING * hidden_units), BF16),
            pltpu.VMEM((RING * total, width // RING), BF16),
            dma((hidden_units // 128 * 2 + 3,)),
        ]
        + [dma((RING,))] * 6
        + [dma((3, 2))] * 2
        + [dma((RING,))] * 2
        + [dma((RING, 3, RING))] * 2
        + [dma((RING, 3, 2))] * 2
        + [dma((RING, RING))] * 2,
        compiler_params=pltpu.CompilerParams(
            collective_id=1, has_side_effects=True, vmem_limit_bytes=VMEM_BYTES
        ),
        name="experts",
    )(packed, meta, gate, up, down)


def mix_kernel(meta, back, state, layer_out, share_out, share_in, matrix, share_send, share_recv, *scratch):
    rows, width = state.shape
    slots = back.shape[0] // RING // RING
    tp, ep = lax.axis_index("tp"), lax.axis_index("ep")
    y, x = ep // RING, ep % RING
    z, core, chips, partner, right, left = tp_place()

    def group_of(block):
        return (block // RING - x + 2 + RING) % RING

    target = (x * RING + tp % RING, y * RING + (x - group_of(tp) + RING) % RING)
    from_x = tp // RING
    shift = (from_x - x + RING) % RING
    source = (((from_x + shift + 2) % RING) * RING + tp % RING, y * RING + from_x)
    greet([partner, right, left, target, source])
    place = lax.broadcasted_iota(jnp.int32, (slots, rows), 0).astype(F32)
    for r in range(RING):
        for d in range(RING):
            slot = meta[pl.ds(r * 2 * RING + d, 1)]
            gate = meta[pl.ds(r * 2 * RING + RING + d, 1)]
            matrix[pl.ds((r * RING + PLACE[d]) * slots, slots)] = jnp.where(slot == place, gate, 0.0).astype(BF16)

    def term(block):
        span = pl.ds(pl.multiple_of(group_of(block) * RING * slots, RING * slots), RING * slots)
        return lax.dot_general(
            matrix[span],
            back[span, columns(block % RING, width)],
            (((0,), (0,)), ((), ())),
            preferred_element_type=F32,
        )

    shares = []

    def give(h, span, total):
        share_out[span] = total.astype(BF16)
        copy = remote(share_out.at[span], share_in.at[span], share_send.at[h], share_recv.at[h], target)
        copy.start()
        shares.append((span, copy))

    sum_over_tp(term, give, scratch)
    for span, copy in shares:
        copy.wait()
        layer_out[span] = (share_in[span].astype(F32) + state[span].astype(F32)).astype(BF16)


def mix(meta, back, state):
    rows, width = state.shape
    return pl.pallas_call(
        mix_kernel,
        out_shape=jax.ShapeDtypeStruct((rows, width), BF16),
        in_specs=in_vmem(3),
        out_specs=pl.BlockSpec(memory_space=pltpu.VMEM),
        scratch_shapes=[
            pltpu.VMEM((rows, width), BF16),
            pltpu.VMEM((rows, width), BF16),
            pltpu.VMEM((back.shape[0], rows), BF16),
            pltpu.SemaphoreType.DMA((2,)),
            pltpu.SemaphoreType.DMA((2,)),
        ]
        + sum_scratch(rows, width),
        compiler_params=pltpu.CompilerParams(
            collective_id=2, has_side_effects=True, vmem_limit_bytes=VMEM_BYTES
        ),
        name="mix",
    )(meta, back, state)


def route(hidden, norm_gain, router_weight, expert_ids, capacity):
    tp, ep = lax.axis_index("tp"), lax.axis_index("ep")
    y = ep // RING
    rows = hidden.shape[0]
    expert_count = router_weight.shape[0]
    state_float = hidden.astype(F32)
    inv_rms = lax.rsqrt(jnp.mean(state_float * state_float, axis=1, keepdims=True) + epsilon)
    normed = (state_float * inv_rms * norm_gain.astype(F32)).astype(BF16)
    logits = lax.dot_general(normed, router_weight, (((1,), (1,)), ((), ())), preferred_element_type=F32)
    every = lax.broadcasted_iota(jnp.int32, (1, 1, expert_count), 2)
    hit_all = jnp.any(expert_ids[:, :, None] == every, axis=1)
    top = jnp.max(jnp.where(hit_all, logits, -jnp.inf), axis=1, keepdims=True)
    raised = jnp.where(hit_all, jnp.exp(jnp.where(hit_all, logits - top, 0.0)), 0.0)
    gates_all = raised / jnp.sum(raised, axis=1, keepdims=True)
    mine = tp * RING + (y + lax.broadcasted_iota(jnp.int32, (1, 1, RING), 2)) % RING
    hit = jnp.any(expert_ids[:, :, None] == mine, axis=1)
    own_gates = jnp.sum(
        jnp.where(lax.broadcasted_iota(jnp.int32, (1, expert_count, 1), 1) == mine, gates_all[:, :, None], 0.0), axis=1
    )
    before = (
        lax.broadcasted_iota(jnp.int32, (rows, rows), 1) <= lax.broadcasted_iota(jnp.int32, (rows, rows), 0)
    ).astype(BF16)
    slot_of = jnp.dot(before, hit.astype(BF16), preferred_element_type=F32).astype(jnp.int32) - 1
    slots = lax.broadcasted_iota(jnp.int32, (1, 1, capacity), 2)
    chosen = (slot_of[:, :, None] == slots) & hit[:, :, None]
    selector = chosen.astype(BF16).reshape(rows, RING * capacity)
    places = jnp.where(hit, slot_of, -1).astype(F32)
    meta = jnp.concatenate([places, own_gates], axis=1).T
    packed = lax.dot_general(
        selector, normed, (((0,), (0,)), ((), ())), preferred_element_type=F32
    ).astype(BF16)
    return packed, meta


def shards(
    context, out_weight, residual, norm_gain, router_weight, expert_ids, w_gate, w_up, w_down
):
    tp = lax.axis_index("tp")
    rows, width = residual.shape
    hidden, spread_down = attend(context, out_weight, residual, w_down[0])
    capacity = min(rows, 2 * rows * expert_ids.shape[1] // router_weight.shape[0])
    packed, meta = route(hidden, norm_gain, router_weight, expert_ids, capacity)
    back, meta_all = experts(packed, meta, w_gate[0], w_up[0], spread_down)
    state = lax.dynamic_slice_in_dim(hidden, tp * width, width, 1)
    return mix(meta_all, back, state)


def solution(mesh):
    in_specs = (
        P("ep", "tp"),
        P("tp", None),
        P("ep", "tp"),
        P(),
        P(),
        P("ep", None),
        P(("tp", "ep"), None, None),
        P(("tp", "ep"), None, None),
        P(("tp", "ep"), None, None),
    )
    out_specs = P("ep", "tp")
    return jax.shard_map(shards, mesh=mesh, in_specs=in_specs, out_specs=out_specs, check_vma=False)
```

```python
import functools

import jax
import jax.numpy as jnp
from jax import lax
from jax.experimental import pallas as pl
from jax.experimental.pallas import tpu as pltpu
from jax.sharding import PartitionSpec as P

SPLIT = 4
RING = 4
epsilon = 1e-06
MESH = pl.DeviceIdType.MESH
F32 = jnp.float32
BF16 = jnp.bfloat16
VMEM_BYTES = 58 * 2**20
PLACE = (3, 0, 2, 1)
STAGES = ((1, 3), (2,), (0,))
ORDER = (0, 1, 7, 2, 6, 3, 5, 4)
GROUPS = ((0, 1, 2), (3, 4), (5, 6, 7))
DISTANCES = (4, 3, 5, 2, 6, 1, 7, 0)


def in_vmem(count):
    return [pl.BlockSpec(memory_space=pltpu.VMEM)] * count


def columns(index, width):
    return pl.ds(pl.multiple_of(index * width, width), width)


def greet(devices):
    barrier = pltpu.get_barrier_semaphore()
    for device in devices:
        pl.semaphore_signal(barrier, inc=1, device_id=device, device_id_type=MESH)
    pl.semaphore_wait(barrier, len(devices))


def remote(source, target, send, recv, device):
    return pltpu.make_async_remote_copy(
        src_ref=source, dst_ref=target, send_sem=send, recv_sem=recv, device_id=device, device_id_type=MESH
    )


def tp_place():
    tp, ep = lax.axis_index("tp"), lax.axis_index("ep")
    chips = lax.axis_size("tp") // 2
    z, core = tp // 2, tp % 2
    partner = (z * 2 + 1 - core, ep)
    right = (((z + 1) % chips) * 2 + core, ep)
    left = (((z + chips - 1) % chips) * 2 + core, ep)
    return z, core, chips, partner, right, left


def sum_scratch(rows, width):
    block = (rows, width)
    return [
        pltpu.VMEM((8, *block), BF16),
        pltpu.VMEM((8, *block), BF16),
        pltpu.VMEM((8, *block), F32),
        pltpu.VMEM((2, 4, *block), BF16),
        pltpu.VMEM((2, 4, *block), BF16),
        pltpu.SemaphoreType.DMA((8,)),
        pltpu.SemaphoreType.DMA((8,)),
        pltpu.SemaphoreType.DMA((2, 4, 2)),
        pltpu.SemaphoreType.DMA((2, 4, 2)),
    ]


def sum_over_tp(term, give, scratch):
    swap_out, swap_in, pairs, arm_out, arm_in, swap_send, swap_recv, arm_send, arm_recv = scratch
    z, core, chips, partner, right, left = tp_place()
    half = swap_out.shape[1] // 2
    spans = (pl.ds(0, half), pl.ds(half, half))
    swaps = {}
    for j in DISTANCES:
        swap_out[j] = term(((z + j) % chips) * 2 + 1 - core).astype(BF16)
        swaps[j] = remote(swap_out.at[j], swap_in.at[j], swap_send.at[j], swap_recv.at[j], partner)
        swaps[j].start()

    def pair(j):
        mine = term(((z + j) % chips) * 2 + core)
        swaps[j].wait_recv()
        pairs[j] = mine + swap_in[j].astype(F32)

    hops = {}

    def hop(arm, h, step):
        value = pairs[4 - step if arm == 0 else 4 + step, spans[h]]
        if (arm, h, step - 1) in hops:
            hops[arm, h, step - 1].wait_recv()
            value = value + arm_in[arm, step - 1, spans[h]].astype(F32)
        arm_out[arm, step, spans[h]] = value.astype(BF16)
        copy = remote(
            arm_out.at[arm, step, spans[h]],
            arm_in.at[arm, step, spans[h]],
            arm_send.at[arm, step, h],
            arm_recv.at[arm, step, h],
            (right, left)[arm],
        )
        copy.start()
        hops[arm, h, step] = copy

    pair(4)
    hop(0, 0, 0)
    hop(1, 1, 0)
    for step in range(1, 4):
        pair(4 - step)
        pair(4 + step)
        hop(0, 1, step)
        hop(1, 0, step)
        hop(0, 0, step)
        hop(1, 1, step)
    pair(0)
    for h in range(2):
        total = pairs[0, spans[h]]
        for arm in (1 - h, h):
            hops[arm, h, 3].wait_recv()
            total = total + arm_in[arm, 3, spans[h]].astype(F32)
        give(h, spans[h], total)
    for copy in list(hops.values()) + list(swaps.values()):
        copy.wait_send()


class GatherOverTp:
    def __init__(self, out, width, sems):
        self.out, self.width = out, width
        self.arm_send, self.arm_recv, self.near_send, self.near_recv = sems
        z, self.core, chips, self.partner, self.right, self.left = tp_place()
        self.half = out.shape[0] // 2
        self.copies = []

    def at(self, j, h, side):
        offset = pl.multiple_of((ORDER.index(j % 8) * 2 + side) * self.width, self.width)
        return self.out.at[pl.ds(h * self.half, self.half), pl.ds(offset, self.width)]

    def go(self, source, target, send, recv, device):
        copy = remote(source, target, send, recv, device)
        copy.start()
        self.copies.append(copy)

    def pass_on(self, arm, h, step):
        sign = 1 if arm else -1
        self.go(
            self.at(sign * step, h, self.core),
            self.at(sign * (step + 1), h, self.core),
            self.arm_send.at[arm, step, h],
            self.arm_recv.at[arm, step, h],
            (self.right, self.left)[arm],
        )

    def to_partner(self, j, h):
        ref = self.at(j, h, self.core)
        self.go(ref, ref, self.near_send.at[j % 8, h], self.near_recv.at[j % 8, h], self.partner)

    def start(self, h):
        for arm in (h, 1 - h):
            self.pass_on(arm, h, 0)
        self.to_partner(0, h)

    def step(self, step):
        for arm, h in ((0, 0), (1, 0), (1, 1), (0, 1)):
            if step == 4 and arm != h:
                continue
            j = step if arm else -step
            ref = self.at(j, h, self.core)
            remote(
                ref, ref, self.arm_send.at[arm, step - 1, h], self.arm_recv.at[arm, step - 1, h], self.right
            ).wait_recv()
            if step < 3 or (step == 3 and arm == h):
                self.pass_on(arm, h, step)
            self.to_partner(j, h)

    def ready(self, j):
        for h in range(2):
            ref = self.at(j, h, 1 - self.core)
            remote(ref, ref, self.near_send.at[j % 8, h], self.near_recv.at[j % 8, h], self.partner).wait_recv()

    def finish(self):
        for copy in self.copies:
            copy.wait_send()


def layer_kernel(
    context, weight, residual, places, gain, router, ids, gate, up, down,
    back, meta_all, state,
    hidden, squares, selector, packed, meta, rows, gate_up, spread, inner, out, *scratch
):
    total_scratch, gather_sems, (spread_send, spread_recv) = scratch[:9], scratch[9:13], scratch[13:15]
    (load, y_send, y_recv, right_send, right_recv, left_send, left_recv, far_send, far_recv, meta_send, meta_recv,
     in_send, in_recv, on_send, on_recv, out_send, out_recv) = scratch[15:]
    tp, ep = lax.axis_index("tp"), lax.axis_index("ep")
    y, x = ep // RING, ep % RING
    z, core, chips, partner, z_right, z_left = tp_place()
    tokens, share = residual.shape
    slots = back.shape[0] // RING // RING
    width = weight.shape[1]
    block = RING * slots
    hidden_units = gate.shape[1]
    pieces = hidden_units // 128
    quarter = width // RING
    pair = 2 * share

    def device(dy, dx):
        return (tp, ((y + dy + RING) % RING) * RING + (x + dx + RING) % RING)

    right, left = device(0, 1), device(0, -1)
    greet(
        [partner, z_right, z_left]
        + [device(0, k) for k in range(1, RING)]
        + [device(k, 0) for k in range(1, RING)]
    )

    def chunk(r, d):
        return pl.ds(r * block + PLACE[d] * slots, slots)

    def unit_span(r, h):
        return pl.ds(r * block + PLACE[STAGES[h][0]] * slots, len(STAGES[h]) * slots)

    def half_span(r, h, side):
        half = len(STAGES[h]) * slots // 2
        return pl.ds(r * block + PLACE[STAGES[h][0]] * slots + side * half, half)

    def inner_columns(k):
        return pl.ds(k * hidden_units, hidden_units)

    copies = []

    def send(source, target, send_sem, recv_sem, to):
        copy = remote(source, target, send_sem, recv_sem, to)
        copy.start()
        copies.append(copy)
        return copy

    spreads = [
        send(
            down.at[:, columns((x + k) % RING, quarter)],
            spread.at[pl.ds(k * hidden_units, hidden_units)],
            spread_send.at[k],
            spread_recv.at[k],
            device(0, k),
        )
        for k in range(1, RING)
    ]
    loads = [(down.at[:, columns(x, quarter)], spread.at[pl.ds(0, hidden_units)])]
    for p, j in enumerate(ORDER):
        source = pl.ds(pl.multiple_of((z + j) % chips * pair, pair), pair)
        target = pl.ds(p * pair, pair)
        for i in range(pieces):
            part = pl.ds(i * 128, 128)
            loads.append((gate.at[source, part], gate_up.at[target, pl.ds(i * 256, 128)]))
            loads.append((up.at[source, part], gate_up.at[target, pl.ds(i * 256 + 128, 128)]))
    loads = [pltpu.make_async_copy(a, b, load.at[i]) for i, (a, b) in enumerate(loads)]
    for copy in loads:
        copy.start()
    place = lax.broadcasted_iota(jnp.int32, (slots, tokens), 0).astype(F32)
    for d in range(RING):
        selector[pl.ds(PLACE[d] * slots, slots)] = jnp.where(places[pl.ds(d, 1)] == place, 1.0, 0.0).astype(BF16)
    squares[...] = jnp.zeros_like(squares)
    gather = GatherOverTp(hidden, share, gather_sems)

    def term(index):
        return jnp.dot(context[...], weight[:, columns(index, share)], preferred_element_type=F32)

    def give(h, span, total):
        mine = (total + residual[span].astype(F32)).astype(BF16)
        state[span] = mine
        hidden[span, columns(core, share)] = mine
        gather.start(h)

    sum_over_tp(term, give, total_scratch)
    y_copies, sides = {}, {}

    def group_columns(g):
        first, last = GROUPS[g][0], GROUPS[g][-1] + 1
        return pl.ds(first * pair, (last - first) * pair + (128 if g == len(GROUPS) - 1 else 0))

    def to_sides(d, g, source):
        part = group_columns(g)
        sides[d, g] = (
            send(source, rows.at[chunk(1, d), part], right_send.at[d, g], right_recv.at[d, g], right),
            send(source, rows.at[chunk(3, d), part], left_send.at[d, g], left_recv.at[d, g], left),
        )

    def y_arrived(d, g):
        y_copies[d, g].wait_recv()
        to_sides(d, g, rows.at[chunk(0, d), group_columns(g)])

    def dispatch(g):
        for p in GROUPS[g]:
            gather.ready(ORDER[p])
            part = pl.ds(p * pair, pair)
            value = hidden[:, part].astype(F32)
            total = squares[...]
            for i in range(pair // 128):
                lanes = value[:, i * 128 : (i + 1) * 128]
                total = total + lanes * lanes
            squares[...] = total
            scaled = (value * gain[:, columns((z + ORDER[p]) % chips, pair)]).astype(BF16)
            packed[:, part] = jnp.dot(selector[...], scaled, preferred_element_type=F32).astype(BF16)
        if g == len(GROUPS) - 1:
            mean = jnp.sum(squares[...], axis=1, keepdims=True) / width
            inverse = lax.rsqrt(mean + epsilon)
            high = inverse.astype(BF16).astype(F32)
            lane = lax.broadcasted_iota(jnp.int32, (tokens, 128), 1)
            parts = jnp.where(lane == 0, high, jnp.where(lane == 1, inverse - high, 0.0)).astype(BF16)
            packed[:, pl.ds(width, 128)] = jnp.dot(selector[...], parts, preferred_element_type=F32).astype(BF16)
        part = group_columns(g)
        for d in (1, 3, 2):
            y_copies[d, g] = send(
                packed.at[chunk(0, d), part], rows.at[chunk(0, d), part], y_send.at[d, g], y_recv.at[d, g], device(d, 0)
            )
        to_sides(0, g, packed.at[chunk(0, 0), part])
        rows[chunk(0, 0), part] = packed[chunk(0, 0), part]

    def unit(r, h):
        span = unit_span(r, h)
        parts = rows[span, pl.ds(width, 128)].astype(F32)
        inverse = parts[:, 0:1] + parts[:, 1:2]

        def step(j, carry):
            both = jnp.dot(rows[span, pl.ds(0, width)], gate_up[:, columns(j, 256)], preferred_element_type=F32)
            both = both * inverse
            value, scale = both[:, :128], both[:, 128:]
            inner[span, columns(j, 128)] = (value / (1.0 + jnp.exp(-value)) * scale).astype(BF16)
            return carry

        lax.fori_loop(0, pieces, step, 0)
        for k in (1, 3):
            there = (r + k) % RING
            send(
                inner.at[span, inner_columns(0)],
                inner.at[unit_span(there, h), inner_columns(k)],
                in_send.at[r, h, k],
                in_recv.at[there, h, k],
                device(0, k),
            )

    def relay(r, h):
        for side, k in ((0, 1), (1, 3)):
            here, there = (r + k) % RING, (r + 2) % RING
            ref = inner.at[unit_span(here, h), inner_columns(k)]
            remote(ref, ref, in_send.at[r, h, k], in_recv.at[here, h, k], right).wait_recv()
            send(
                inner.at[half_span(here, h, side), inner_columns(k)],
                inner.at[half_span(there, h, side), inner_columns(2)],
                on_send.at[r, h, side],
                on_recv.at[there, h, side],
                (right, left)[side],
            )

    def came_right(d):
        for g in range(len(GROUPS)):
            sides[d, g][0].wait_recv()

    def came_left(d):
        for g in range(len(GROUPS)):
            sides[d, g][1].wait_recv()

    far = {}

    def onward(h, side):
        far[h, side] = send(
            rows.at[half_span((1, 3)[side], h, side)],
            rows.at[half_span(2, h, side)],
            far_send.at[h, side],
            far_recv.at[h, side],
            (right, left)[side],
        )

    def came_far(h):
        far[h, 0].wait_recv()
        far[h, 1].wait_recv()

    def finish(r, h):
        span = unit_span(r, h)
        for side in range(2):
            ref = inner.at[half_span(r, h, side), inner_columns(2)]
            remote(ref, ref, on_send.at[r, h, side], on_recv.at[r, h, side], right).wait_recv()

        def step(n, carry):
            out[span, columns(n, 256)] = jnp.dot(
                inner[span], spread[:, columns(n, 256)], preferred_element_type=F32
            ).astype(BF16)
            return carry

        lax.fori_loop(0, quarter // 256, step, 0)
        for d in STAGES[h]:
            target = back.at[chunk(r, d)]
            if d == 0:
                copy = pltpu.make_async_copy(out.at[chunk(r, 0)], target, out_send.at[r, 0])
                copy.start()
                kept.append(copy)
            else:
                send(out.at[chunk(r, d)], target, out_send.at[r, d], out_recv.at[r, d], device(-d, 0))

    def gates():
        inverse = lax.rsqrt(jnp.sum(squares[...], axis=1, keepdims=True) / width + epsilon)
        count = router.shape[0]
        logits = jnp.zeros((tokens, count), F32)
        for p, j in enumerate(ORDER):
            part = columns((z + j) % chips, pair)
            normed = (hidden[:, pl.ds(p * pair, pair)].astype(F32) * inverse * gain[:, part]).astype(BF16)
            logits = logits + lax.dot_general(
                normed, router[:, part], (((1,), (1,)), ((), ())), preferred_element_type=F32
            )
        every = lax.broadcasted_iota(jnp.int32, (tokens, count), 1)
        hit = every == ids[:, 0:1]
        for k in range(1, ids.shape[1]):
            hit = hit | (every == ids[:, k : k + 1])
        top = jnp.max(jnp.where(hit, logits, -jnp.inf), axis=1, keepdims=True)
        raised = jnp.where(hit, jnp.exp(jnp.where(hit, logits - top, 0.0)), 0.0)
        softmax = raised / jnp.sum(raised, axis=1, keepdims=True)
        lane = lax.broadcasted_iota(jnp.int32, (tokens, 128), 1)
        own = jnp.zeros((tokens, 128), F32)
        for d in range(RING):
            value = jnp.sum(jnp.where(every == tp * RING + (y + d) % RING, softmax, 0.0), axis=1, keepdims=True)
            own = own + jnp.where(lane == d, value, 0.0)
        meta[pl.ds(0, RING)] = places[pl.ds(0, RING)]
        meta[pl.ds(RING, RING)] = own.T[:RING]

    gather.step(1)
    dispatch(0)
    gather.step(2)
    dispatch(1)
    y_arrived(1, 0)
    y_arrived(3, 0)
    gather.step(3)
    gather.step(4)
    dispatch(2)
    y_arrived(1, 1)
    y_arrived(3, 1)
    gates()
    meta_all[pl.ds(0, 2 * RING)] = meta[...]
    metas = [
        send(meta, meta_all.at[pl.ds(k * 2 * RING, 2 * RING)], meta_send.at[k], meta_recv.at[k], device(0, k))
        for k in range(1, RING)
    ]
    y_arrived(1, 2)
    y_arrived(3, 2)
    for copy in loads:
        copy.wait()
    kept = []
    unit(0, 0)
    came_right(0)
    came_left(0)
    unit(0, 2)
    for g in range(3):
        y_arrived(2, g)
    came_right(1)
    onward(0, 0)
    came_left(3)
    onward(0, 1)
    came_left(1)
    came_right(3)
    unit(1, 0)
    unit(3, 0)
    relay(0, 0)
    unit(1, 2)
    unit(3, 2)
    unit(0, 1)
    came_right(2)
    onward(1, 0)
    came_left(2)
    onward(1, 1)
    relay(1, 0)
    relay(3, 0)
    came_far(0)
    unit(2, 0)
    onward(2, 0)
    onward(2, 1)
    unit(1, 1)
    unit(3, 1)
    relay(0, 1)
    relay(0, 2)
    relay(2, 0)
    for copy in spreads:
        copy.wait_recv()
    for r in (0, 1, 3, 2):
        finish(r, 0)
    relay(1, 1)
    relay(3, 1)
    came_far(1)
    unit(2, 1)
    relay(1, 2)
    relay(3, 2)
    came_far(2)
    unit(2, 2)
    relay(2, 1)
    for r in (0, 1, 3, 2):
        finish(r, 1)
    relay(2, 2)
    for r in (0, 1, 3, 2):
        finish(r, 2)
    for copy in kept:
        copy.wait()
    for r in range(RING):
        for d in range(1, RING):
            ref = back.at[chunk(r, d)]
            remote(ref, ref, out_send.at[r, d], out_recv.at[r, d], device(d, 0)).wait_recv()
    for copy in metas:
        copy.wait_recv()
    gather.finish()
    for copy in copies:
        copy.wait_send()


def layer(context, weight, residual, places, gain, router, ids, gate, up, down, slots):
    tokens, share = residual.shape
    width, hidden_units = gate.shape
    total = RING * slots
    dma = pltpu.SemaphoreType.DMA
    return pl.pallas_call(
        layer_kernel,
        out_shape=(
            jax.ShapeDtypeStruct((RING * total, width // RING), BF16),
            jax.ShapeDtypeStruct((RING * 2 * RING, tokens), F32),
            jax.ShapeDtypeStruct((tokens, share), BF16),
        ),
        in_specs=in_vmem(7) + [pl.BlockSpec(memory_space=pl.ANY)] * 3,
        out_specs=tuple(in_vmem(3)),
        scratch_shapes=[
            pltpu.VMEM((tokens, width), BF16),
            pltpu.VMEM((tokens, 128), F32),
            pltpu.VMEM((total, tokens), BF16),
            pltpu.VMEM((total, width + 128), BF16),
            pltpu.VMEM((2 * RING, tokens), F32),
            pltpu.VMEM((RING * total, width + 128), BF16),
            pltpu.VMEM((width, 2 * hidden_units), BF16),
            pltpu.VMEM((RING * hidden_units, width // RING), BF16),
            pltpu.VMEM((RING * total, RING * hidden_units), BF16),
            pltpu.VMEM((RING * total, width // RING), BF16),
        ]
        + sum_scratch(tokens, share)
        + [dma((2, 4, 2))] * 2
        + [dma((8, 2))] * 2
        + [dma((RING,))] * 2
        + [dma((hidden_units // 128 * 16 + 1,))]
        + [dma((RING, 3))] * 6
        + [dma((3, 2))] * 2
        + [dma((RING,))] * 2
        + [dma((RING, 3, RING))] * 2
        + [dma((RING, 3, 2))] * 2
        + [dma((RING, RING))] * 2,
        compiler_params=pltpu.CompilerParams(
            collective_id=0, has_side_effects=True, vmem_limit_bytes=VMEM_BYTES
        ),
        name="layer",
    )(context, weight, residual, places, gain, router, ids, gate, up, down)


def mix_kernel(meta, back, state, layer_out, share_out, share_in, matrix, share_send, share_recv, *scratch):
    rows, width = state.shape
    slots = back.shape[0] // RING // RING
    tp, ep = lax.axis_index("tp"), lax.axis_index("ep")
    y, x = ep // RING, ep % RING
    z, core, chips, partner, right, left = tp_place()

    def group_of(block):
        return (block // RING - x + 2 + RING) % RING

    target = (x * RING + tp % RING, y * RING + (x - group_of(tp) + RING) % RING)
    from_x = tp // RING
    shift = (from_x - x + RING) % RING
    source = (((from_x + shift + 2) % RING) * RING + tp % RING, y * RING + from_x)
    greet([partner, right, left, target, source])
    place = lax.broadcasted_iota(jnp.int32, (slots, rows), 0).astype(F32)
    for r in range(RING):
        for d in range(RING):
            slot = meta[pl.ds(r * 2 * RING + d, 1)]
            gate = meta[pl.ds(r * 2 * RING + RING + d, 1)]
            matrix[pl.ds((r * RING + PLACE[d]) * slots, slots)] = jnp.where(slot == place, gate, 0.0).astype(BF16)

    def term(block):
        span = pl.ds(pl.multiple_of(group_of(block) * RING * slots, RING * slots), RING * slots)
        return lax.dot_general(
            matrix[span],
            back[span, columns(block % RING, width)],
            (((0,), (0,)), ((), ())),
            preferred_element_type=F32,
        )

    shares = []

    def give(h, span, total):
        share_out[span] = total.astype(BF16)
        copy = remote(share_out.at[span], share_in.at[span], share_send.at[h], share_recv.at[h], target)
        copy.start()
        shares.append((span, copy))

    sum_over_tp(term, give, scratch)
    for span, copy in shares:
        copy.wait()
        layer_out[span] = (share_in[span].astype(F32) + state[span].astype(F32)).astype(BF16)


def mix(meta, back, state):
    rows, width = state.shape
    return pl.pallas_call(
        mix_kernel,
        out_shape=jax.ShapeDtypeStruct((rows, width), BF16),
        in_specs=in_vmem(3),
        out_specs=pl.BlockSpec(memory_space=pltpu.VMEM),
        scratch_shapes=[
            pltpu.VMEM((rows, width), BF16),
            pltpu.VMEM((rows, width), BF16),
            pltpu.VMEM((back.shape[0], rows), BF16),
            pltpu.SemaphoreType.DMA((2,)),
            pltpu.SemaphoreType.DMA((2,)),
        ]
        + sum_scratch(rows, width),
        compiler_params=pltpu.CompilerParams(
            collective_id=1, has_side_effects=True, vmem_limit_bytes=VMEM_BYTES
        ),
        name="mix",
    )(meta, back, state)


def slots_of(expert_ids):
    tp, ep = lax.axis_index("tp"), lax.axis_index("ep")
    rows = expert_ids.shape[0]
    mine = tp * RING + (ep // RING + lax.broadcasted_iota(jnp.int32, (1, RING, 1), 1)) % RING
    hit = jnp.any(expert_ids.T[:, None, :] == mine.reshape(1, RING, 1), axis=0)
    upto = (
        lax.broadcasted_iota(jnp.int32, (rows, rows), 0) <= lax.broadcasted_iota(jnp.int32, (rows, rows), 1)
    ).astype(BF16)
    count = jnp.dot(hit.astype(BF16), upto, preferred_element_type=F32)
    places = jnp.where(hit, count - 1.0, -1.0)
    return jnp.concatenate([places, places], axis=0)


def shards(
    context, out_weight, residual, norm_gain, router_weight, expert_ids, w_gate, w_up, w_down
):
    rows = residual.shape[0]
    capacity = min(rows, 2 * rows * expert_ids.shape[1] // router_weight.shape[0])
    back, meta_all, state = layer(
        context,
        out_weight,
        residual,
        slots_of(expert_ids),
        norm_gain.astype(F32)[None],
        router_weight,
        expert_ids,
        w_gate[0],
        w_up[0],
        w_down[0],
        capacity,
    )
    return mix(meta_all, back, state)


def solution(mesh):
    in_specs = (
        P("ep", "tp"),
        P("tp", None),
        P("ep", "tp"),
        P(),
        P(),
        P("ep", None),
        P(("tp", "ep"), None, None),
        P(("tp", "ep"), None, None),
        P(("tp", "ep"), None, None),
    )
    out_specs = P("ep", "tp")
    return jax.shard_map(shards, mesh=mesh, in_specs=in_specs, out_specs=out_specs, check_vma=False)
```

```python
import functools

import jax
import jax.numpy as jnp
from jax import lax
from jax.experimental import pallas as pl
from jax.experimental.pallas import tpu as pltpu
from jax.sharding import PartitionSpec as P

SPLIT = 4
RING = 4
epsilon = 1e-06
MESH = pl.DeviceIdType.MESH
F32 = jnp.float32
BF16 = jnp.bfloat16
VMEM_BYTES = 58 * 2**20
PLACE = (3, 0, 2, 1)
STAGES = ((1, 3), (2,), (0,))
ORDER = (0, 1, 7, 2, 6, 3, 5, 4)
GROUPS = ((0, 1, 2), (3, 4), (5, 6, 7))
DISTANCES = (4, 3, 5, 2, 6, 1, 7, 0)


def in_vmem(count):
    return [pl.BlockSpec(memory_space=pltpu.VMEM)] * count


def columns(index, width):
    return pl.ds(pl.multiple_of(index * width, width), width)


def greet(devices):
    barrier = pltpu.get_barrier_semaphore()
    for device in devices:
        pl.semaphore_signal(barrier, inc=1, device_id=device, device_id_type=MESH)
    pl.semaphore_wait(barrier, len(devices))


def remote(source, target, send, recv, device):
    return pltpu.make_async_remote_copy(
        src_ref=source, dst_ref=target, send_sem=send, recv_sem=recv, device_id=device, device_id_type=MESH
    )


def tp_place():
    tp, ep = lax.axis_index("tp"), lax.axis_index("ep")
    chips = lax.axis_size("tp") // 2
    z, core = tp // 2, tp % 2
    partner = (z * 2 + 1 - core, ep)
    right = (((z + 1) % chips) * 2 + core, ep)
    left = (((z + chips - 1) % chips) * 2 + core, ep)
    return z, core, chips, partner, right, left


def sum_scratch(rows, width):
    block = (rows, width)
    return [
        pltpu.VMEM((8, *block), BF16),
        pltpu.VMEM((8, *block), BF16),
        pltpu.VMEM((8, *block), F32),
        pltpu.VMEM((2, 4, *block), BF16),
        pltpu.VMEM((2, 4, *block), BF16),
        pltpu.SemaphoreType.DMA((8,)),
        pltpu.SemaphoreType.DMA((8,)),
        pltpu.SemaphoreType.DMA((2, 4, 2)),
        pltpu.SemaphoreType.DMA((2, 4, 2)),
    ]


def sum_over_tp(term, give, scratch):
    swap_out, swap_in, pairs, arm_out, arm_in, swap_send, swap_recv, arm_send, arm_recv = scratch
    z, core, chips, partner, right, left = tp_place()
    half = swap_out.shape[1] // 2
    spans = (pl.ds(0, half), pl.ds(half, half))
    swaps = {}
    for j in DISTANCES:
        swap_out[j] = term(((z + j) % chips) * 2 + 1 - core).astype(BF16)
        swaps[j] = remote(swap_out.at[j], swap_in.at[j], swap_send.at[j], swap_recv.at[j], partner)
        swaps[j].start()

    def pair(j):
        mine = term(((z + j) % chips) * 2 + core)
        swaps[j].wait_recv()
        pairs[j] = mine + swap_in[j].astype(F32)

    hops = {}

    def hop(arm, h, step):
        value = pairs[4 - step if arm == 0 else 4 + step, spans[h]]
        if (arm, h, step - 1) in hops:
            hops[arm, h, step - 1].wait_recv()
            value = value + arm_in[arm, step - 1, spans[h]].astype(F32)
        arm_out[arm, step, spans[h]] = value.astype(BF16)
        copy = remote(
            arm_out.at[arm, step, spans[h]],
            arm_in.at[arm, step, spans[h]],
            arm_send.at[arm, step, h],
            arm_recv.at[arm, step, h],
            (right, left)[arm],
        )
        copy.start()
        hops[arm, h, step] = copy

    pair(4)
    hop(0, 0, 0)
    hop(1, 1, 0)
    for step in range(1, 4):
        pair(4 - step)
        pair(4 + step)
        hop(0, 1, step)
        hop(1, 0, step)
        hop(0, 0, step)
        hop(1, 1, step)
    pair(0)
    for h in range(2):
        total = pairs[0, spans[h]]
        for arm in (1 - h, h):
            hops[arm, h, 3].wait_recv()
            total = total + arm_in[arm, 3, spans[h]].astype(F32)
        give(h, spans[h], total)
    for copy in list(hops.values()) + list(swaps.values()):
        copy.wait_send()


class GatherOverTp:
    def __init__(self, out, width, sems):
        self.out, self.width = out, width
        self.arm_send, self.arm_recv, self.near_send, self.near_recv = sems
        z, self.core, chips, self.partner, self.right, self.left = tp_place()
        self.half = out.shape[0] // 2
        self.copies = []

    def at(self, j, h, side):
        offset = pl.multiple_of((ORDER.index(j % 8) * 2 + side) * self.width, self.width)
        return self.out.at[pl.ds(h * self.half, self.half), pl.ds(offset, self.width)]

    def go(self, source, target, send, recv, device):
        copy = remote(source, target, send, recv, device)
        copy.start()
        self.copies.append(copy)

    def pass_on(self, arm, h, step):
        sign = 1 if arm else -1
        self.go(
            self.at(sign * step, h, self.core),
            self.at(sign * (step + 1), h, self.core),
            self.arm_send.at[arm, step, h],
            self.arm_recv.at[arm, step, h],
            (self.right, self.left)[arm],
        )

    def to_partner(self, j, h):
        ref = self.at(j, h, self.core)
        self.go(ref, ref, self.near_send.at[j % 8, h], self.near_recv.at[j % 8, h], self.partner)

    def start(self, h):
        for arm in (h, 1 - h):
            self.pass_on(arm, h, 0)
        self.to_partner(0, h)

    def step(self, step):
        for arm, h in ((0, 0), (1, 0), (1, 1), (0, 1)):
            if step == 4 and arm != h:
                continue
            j = step if arm else -step
            ref = self.at(j, h, self.core)
            remote(
                ref, ref, self.arm_send.at[arm, step - 1, h], self.arm_recv.at[arm, step - 1, h], self.right
            ).wait_recv()
            if step < 3 or (step == 3 and arm == h):
                self.pass_on(arm, h, step)
            self.to_partner(j, h)

    def ready(self, j):
        for h in range(2):
            ref = self.at(j, h, 1 - self.core)
            remote(ref, ref, self.near_send.at[j % 8, h], self.near_recv.at[j % 8, h], self.partner).wait_recv()

    def finish(self):
        for copy in self.copies:
            copy.wait_send()


def layer_kernel(
    context, weight, residual, places, gain, router, ids, gate, up, down,
    back, meta_all, state,
    hidden, dense, squares, places_all, selector, packed, packed_far, meta, rows, gate_up, spread, inner, out, *scratch
):
    total_scratch, gather_sems, (spread_send, spread_recv) = scratch[:9], scratch[9:13], scratch[13:15]
    (load, y_send, y_recv, right_send, right_recv, left_send, left_recv, far_send, far_recv, meta_send, meta_recv,
     in_send, in_recv, on_send, on_recv, out_send, out_recv,
     place_send, place_recv, dense_send, dense_recv, beyond_send, beyond_recv) = scratch[15:]
    tp, ep = lax.axis_index("tp"), lax.axis_index("ep")
    y, x = ep // RING, ep % RING
    z, core, chips, partner, z_right, z_left = tp_place()
    tokens, share = residual.shape
    slots = back.shape[0] // RING // RING
    width = weight.shape[1]
    block = RING * slots
    hidden_units = gate.shape[1]
    pieces = hidden_units // 128
    quarter = width // RING
    pair = 2 * share
    early = GROUPS[2][0] * pair
    late = pl.ds(early, width + 128 - early)

    def device(dy, dx):
        return (tp, ((y + dy + RING) % RING) * RING + (x + dx + RING) % RING)

    right, left = device(0, 1), device(0, -1)
    greet(
        [partner, z_right, z_left]
        + [device(0, k) for k in range(1, RING)]
        + [device(k, 0) for k in range(1, RING)]
    )

    def chunk(r, d):
        return pl.ds(r * block + PLACE[d] * slots, slots)

    def unit_span(r, h):
        return pl.ds(r * block + PLACE[STAGES[h][0]] * slots, len(STAGES[h]) * slots)

    def half_span(r, h, side):
        half = len(STAGES[h]) * slots // 2
        return pl.ds(r * block + PLACE[STAGES[h][0]] * slots + side * half, half)

    def inner_columns(k):
        return pl.ds(k * hidden_units, hidden_units)

    copies = []

    def send(source, target, send_sem, recv_sem, to):
        copy = remote(source, target, send_sem, recv_sem, to)
        copy.start()
        copies.append(copy)
        return copy

    spreads = [
        send(
            down.at[:, columns((x + k) % RING, quarter)],
            spread.at[pl.ds(k * hidden_units, hidden_units)],
            spread_send.at[k],
            spread_recv.at[k],
            device(0, k),
        )
        for k in range(1, RING)
    ]
    place_copies = [
        send(places, places_all.at[pl.ds(k * 2 * RING, 2 * RING)], place_send.at[k], place_recv.at[k], device(0, k))
        for k in range(1, RING)
    ]
    loads = [(down.at[:, columns(x, quarter)], spread.at[pl.ds(0, hidden_units)])]
    for p, j in enumerate(ORDER):
        source = pl.ds(pl.multiple_of((z + j) % chips * pair, pair), pair)
        target = pl.ds(p * pair, pair)
        for i in range(pieces):
            part = pl.ds(i * 128, 128)
            loads.append((gate.at[source, part], gate_up.at[target, pl.ds(i * 256, 128)]))
            loads.append((up.at[source, part], gate_up.at[target, pl.ds(i * 256 + 128, 128)]))
    loads = [pltpu.make_async_copy(a, b, load.at[i]) for i, (a, b) in enumerate(loads)]
    for copy in loads:
        copy.start()
    place = lax.broadcasted_iota(jnp.int32, (slots, tokens), 0).astype(F32)

    def select(r, source, first):
        for d in range(RING):
            hit = source[pl.ds(first + d, 1)] == place
            selector[pl.ds(r * block + PLACE[d] * slots, slots)] = jnp.where(hit, 1.0, 0.0).astype(BF16)

    select(0, places, 0)
    squares[...] = jnp.zeros_like(squares)
    gather = GatherOverTp(hidden, share, gather_sems)

    def term(index):
        return jnp.dot(context[...], weight[:, columns(index, share)], preferred_element_type=F32)

    def give(h, span, total):
        mine = (total + residual[span].astype(F32)).astype(BF16)
        state[span] = mine
        hidden[span, columns(core, share)] = mine
        gather.start(h)

    sum_over_tp(term, give, total_scratch)
    y_copies, sides, denses, far_copies = {}, {}, {}, {}

    def group_columns(g):
        first, last = GROUPS[g][0], GROUPS[g][-1] + 1
        return pl.ds(first * pair, (last - first) * pair + (128 if g == len(GROUPS) - 1 else 0))

    def to_sides(d, g, source):
        part = group_columns(g)
        sides[d, g] = (
            send(source, rows.at[chunk(1, d), part], right_send.at[d, g], right_recv.at[d, g], right),
            send(source, rows.at[chunk(3, d), part], left_send.at[d, g], left_recv.at[d, g], left),
        )

    def y_arrived(d, g):
        y_copies[d, g].wait_recv()
        if g < 2:
            to_sides(d, g, rows.at[chunk(0, d), group_columns(g)])

    def dispatch(g):
        for p in GROUPS[g]:
            gather.ready(ORDER[p])
            part = pl.ds(p * pair, pair)
            value = hidden[:, part].astype(F32)
            total = squares[...]
            for i in range(pair // 128):
                lanes = value[:, i * 128 : (i + 1) * 128]
                total = total + lanes * lanes
            squares[...] = total
            scaled = (value * gain[:, columns((z + ORDER[p]) % chips, pair)]).astype(BF16)
            packed[:, part] = jnp.dot(selector[pl.ds(0, block)], scaled, preferred_element_type=F32).astype(BF16)
        if g == len(GROUPS) - 1:
            mean = jnp.sum(squares[...], axis=1, keepdims=True) / width
            inverse = lax.rsqrt(mean + epsilon)
            high = inverse.astype(BF16).astype(F32)
            lane = lax.broadcasted_iota(jnp.int32, (tokens, 128), 1)
            parts = jnp.where(lane == 0, high, jnp.where(lane == 1, inverse - high, 0.0)).astype(BF16)
            hidden[:, pl.ds(width, 128)] = parts
            packed[:, pl.ds(width, 128)] = jnp.dot(
                selector[pl.ds(0, block)], parts, preferred_element_type=F32
            ).astype(BF16)
            denses[1] = send(hidden.at[:, late], dense.at[pl.ds(0, tokens)], dense_send.at[1], dense_recv.at[1], right)
            denses[3] = send(
                hidden.at[:, late], dense.at[pl.ds(2 * tokens, tokens)], dense_send.at[3], dense_recv.at[3], left
            )
        part = group_columns(g)
        for d in (1, 3, 2):
            y_copies[d, g] = send(
                packed.at[chunk(0, d), part], rows.at[chunk(0, d), part], y_send.at[d, g], y_recv.at[d, g], device(d, 0)
            )
        if g < 2:
            to_sides(0, g, packed.at[chunk(0, 0), part])
        rows[chunk(0, 0), part] = packed[chunk(0, 0), part]

    def dense_onward(side):
        half = tokens // 2
        r = (1, 3)[side]
        denses[r].wait_recv()
        denses[2, side] = send(
            dense.at[pl.ds((r - 1) * tokens + side * half, half)],
            dense.at[pl.ds(tokens + side * half, half)],
            beyond_send.at[side],
            beyond_recv.at[side],
            (right, left)[side],
        )

    def pack_far(r):
        place_copies[r - 1].wait_recv()
        select(r, places_all, r * 2 * RING)
        chosen = selector[pl.ds(r * block, block)]
        span, target = pl.ds((r - 1) * tokens, tokens), pl.ds((r - 1) * block, block)
        for p in GROUPS[2]:
            part = pl.ds(p * pair - early, pair)
            scaled = (dense[span, part].astype(F32) * gain[:, columns((z + ORDER[p]) % chips, pair)]).astype(BF16)
            packed_far[target, part] = jnp.dot(chosen, scaled, preferred_element_type=F32).astype(BF16)
        part = pl.ds(width - early, 128)
        packed_far[target, part] = jnp.dot(chosen, dense[span, part], preferred_element_type=F32).astype(BF16)
        for d in (1, 3, 2):
            far_copies[r, d] = send(
                packed_far.at[chunk(r - 1, d)], rows.at[chunk(r, d), late], y_send.at[d, r + 2], y_recv.at[d, r + 2], device(d, 0)
            )
        rows[chunk(r, 0), late] = packed_far[chunk(r - 1, 0)]

    def unit(r, h):
        for d in STAGES[h]:
            if r and d:
                far_copies[r, d].wait_recv()
        span = unit_span(r, h)
        parts = rows[span, pl.ds(width, 128)].astype(F32)
        inverse = parts[:, 0:1] + parts[:, 1:2]

        def step(j, carry):
            both = jnp.dot(rows[span, pl.ds(0, width)], gate_up[:, columns(j, 256)], preferred_element_type=F32)
            both = both * inverse
            value, scale = both[:, :128], both[:, 128:]
            inner[span, columns(j, 128)] = (value / (1.0 + jnp.exp(-value)) * scale).astype(BF16)
            return carry

        lax.fori_loop(0, pieces, step, 0)
        for k in (1, 3):
            there = (r + k) % RING
            send(
                inner.at[span, inner_columns(0)],
                inner.at[unit_span(there, h), inner_columns(k)],
                in_send.at[r, h, k],
                in_recv.at[there, h, k],
                device(0, k),
            )

    def relay(r, h):
        for side, k in ((0, 1), (1, 3)):
            here, there = (r + k) % RING, (r + 2) % RING
            ref = inner.at[unit_span(here, h), inner_columns(k)]
            remote(ref, ref, in_send.at[r, h, k], in_recv.at[here, h, k], right).wait_recv()
            send(
                inner.at[half_span(here, h, side), inner_columns(k)],
                inner.at[half_span(there, h, side), inner_columns(2)],
                on_send.at[r, h, side],
                on_recv.at[there, h, side],
                (right, left)[side],
            )

    def came_right(d):
        for g in range(2):
            sides[d, g][0].wait_recv()

    def came_left(d):
        for g in range(2):
            sides[d, g][1].wait_recv()

    far = {}

    def onward(h, side):
        far[h, side] = send(
            rows.at[half_span((1, 3)[side], h, side), pl.ds(0, early)],
            rows.at[half_span(2, h, side), pl.ds(0, early)],
            far_send.at[h, side],
            far_recv.at[h, side],
            (right, left)[side],
        )

    def came_far(h):
        far[h, 0].wait_recv()
        far[h, 1].wait_recv()

    def finish(r, h):
        span = unit_span(r, h)
        for side in range(2):
            ref = inner.at[half_span(r, h, side), inner_columns(2)]
            remote(ref, ref, on_send.at[r, h, side], on_recv.at[r, h, side], right).wait_recv()

        def step(n, carry):
            out[span, columns(n, 256)] = jnp.dot(
                inner[span], spread[:, columns(n, 256)], preferred_element_type=F32
            ).astype(BF16)
            return carry

        lax.fori_loop(0, quarter // 256, step, 0)
        for d in STAGES[h]:
            target = back.at[chunk(r, d)]
            if d == 0:
                copy = pltpu.make_async_copy(out.at[chunk(r, 0)], target, out_send.at[r, 0])
                copy.start()
                kept.append(copy)
            else:
                send(out.at[chunk(r, d)], target, out_send.at[r, d], out_recv.at[r, d], device(-d, 0))

    def gates():
        inverse = lax.rsqrt(jnp.sum(squares[...], axis=1, keepdims=True) / width + epsilon)
        count = router.shape[0]
        logits = jnp.zeros((tokens, count), F32)
        for p, j in enumerate(ORDER):
            part = columns((z + j) % chips, pair)
            normed = (hidden[:, pl.ds(p * pair, pair)].astype(F32) * inverse * gain[:, part]).astype(BF16)
            logits = logits + lax.dot_general(
                normed, router[:, part], (((1,), (1,)), ((), ())), preferred_element_type=F32
            )
        every = lax.broadcasted_iota(jnp.int32, (tokens, count), 1)
        hit = every == ids[:, 0:1]
        for k in range(1, ids.shape[1]):
            hit = hit | (every == ids[:, k : k + 1])
        top = jnp.max(jnp.where(hit, logits, -jnp.inf), axis=1, keepdims=True)
        raised = jnp.where(hit, jnp.exp(jnp.where(hit, logits - top, 0.0)), 0.0)
        softmax = raised / jnp.sum(raised, axis=1, keepdims=True)
        lane = lax.broadcasted_iota(jnp.int32, (tokens, 128), 1)
        own = jnp.zeros((tokens, 128), F32)
        for d in range(RING):
            value = jnp.sum(jnp.where(every == tp * RING + (y + d) % RING, softmax, 0.0), axis=1, keepdims=True)
            own = own + jnp.where(lane == d, value, 0.0)
        meta[pl.ds(0, RING)] = places[pl.ds(0, RING)]
        meta[pl.ds(RING, RING)] = own.T[:RING]

    gather.step(1)
    dispatch(0)
    gather.step(2)
    dispatch(1)
    y_arrived(1, 0)
    y_arrived(3, 0)
    gather.step(3)
    gather.step(4)
    dispatch(2)
    y_arrived(1, 1)
    y_arrived(3, 1)
    gates()
    meta_all[pl.ds(0, 2 * RING)] = meta[...]
    metas = [
        send(meta, meta_all.at[pl.ds(k * 2 * RING, 2 * RING)], meta_send.at[k], meta_recv.at[k], device(0, k))
        for k in range(1, RING)
    ]
    y_arrived(1, 2)
    y_arrived(3, 2)
    for copy in loads:
        copy.wait()
    kept = []
    unit(0, 0)
    unit(0, 2)
    for g in range(3):
        y_arrived(2, g)
    dense_onward(0)
    dense_onward(1)
    pack_far(1)
    pack_far(3)
    came_right(0)
    came_left(0)
    came_right(1)
    onward(0, 0)
    came_left(3)
    onward(0, 1)
    came_left(1)
    came_right(3)
    denses[2, 0].wait_recv()
    denses[2, 1].wait_recv()
    pack_far(2)
    unit(1, 0)
    unit(3, 0)
    relay(0, 0)
    unit(1, 2)
    unit(3, 2)
    unit(0, 1)
    came_right(2)
    onward(1, 0)
    came_left(2)
    onward(1, 1)
    relay(1, 0)
    relay(3, 0)
    came_far(0)
    unit(2, 0)
    onward(2, 0)
    onward(2, 1)
    unit(1, 1)
    unit(3, 1)
    relay(0, 1)
    relay(0, 2)
    relay(2, 0)
    for copy in spreads:
        copy.wait_recv()
    for r in (0, 1, 3, 2):
        finish(r, 0)
    relay(1, 1)
    relay(3, 1)
    came_far(1)
    unit(2, 1)
    relay(1, 2)
    relay(3, 2)
    came_far(2)
    unit(2, 2)
    relay(2, 1)
    for r in (0, 1, 3, 2):
        finish(r, 1)
    relay(2, 2)
    for r in (0, 1, 3, 2):
        finish(r, 2)
    for copy in kept:
        copy.wait()
    for r in range(RING):
        for d in range(1, RING):
            ref = back.at[chunk(r, d)]
            remote(ref, ref, out_send.at[r, d], out_recv.at[r, d], device(d, 0)).wait_recv()
    for copy in metas:
        copy.wait_recv()
    gather.finish()
    for copy in copies:
        copy.wait_send()


def layer(context, weight, residual, places, gain, router, ids, gate, up, down, slots):
    tokens, share = residual.shape
    width, hidden_units = gate.shape
    total = RING * slots
    late = width + 128 - GROUPS[2][0] * 2 * share
    dma = pltpu.SemaphoreType.DMA
    return pl.pallas_call(
        layer_kernel,
        out_shape=(
            jax.ShapeDtypeStruct((RING * total, width // RING), BF16),
            jax.ShapeDtypeStruct((RING * 2 * RING, tokens), F32),
            jax.ShapeDtypeStruct((tokens, share), BF16),
        ),
        in_specs=in_vmem(7) + [pl.BlockSpec(memory_space=pl.ANY)] * 3,
        out_specs=tuple(in_vmem(3)),
        scratch_shapes=[
            pltpu.VMEM((tokens, width + 128), BF16),
            pltpu.VMEM((3 * tokens, late), BF16),
            pltpu.VMEM((tokens, 128), F32),
            pltpu.VMEM((RING * 2 * RING, tokens), F32),
            pltpu.VMEM((RING * total, tokens), BF16),
            pltpu.VMEM((total, width + 128), BF16),
            pltpu.VMEM((3 * total, late), BF16),
            pltpu.VMEM((2 * RING, tokens), F32),
            pltpu.VMEM((RING * total, width + 128), BF16),
            pltpu.VMEM((width, 2 * hidden_units), BF16),
            pltpu.VMEM((RING * hidden_units, width // RING), BF16),
            pltpu.VMEM((RING * total, RING * hidden_units), BF16),
            pltpu.VMEM((RING * total, width // RING), BF16),
        ]
        + sum_scratch(tokens, share)
        + [dma((2, 4, 2))] * 2
        + [dma((8, 2))] * 2
        + [dma((RING,))] * 2
        + [dma((hidden_units // 128 * 16 + 1,))]
        + [dma((RING, 6))] * 2
        + [dma((RING, 3))] * 4
        + [dma((3, 2))] * 2
        + [dma((RING,))] * 2
        + [dma((RING, 3, RING))] * 2
        + [dma((RING, 3, 2))] * 2
        + [dma((RING, RING))] * 2
        + [dma((RING,))] * 4
        + [dma((2,))] * 2,
        compiler_params=pltpu.CompilerParams(
            collective_id=0, has_side_effects=True, vmem_limit_bytes=VMEM_BYTES
        ),
        name="layer",
    )(context, weight, residual, places, gain, router, ids, gate, up, down)


def mix_kernel(meta, back, state, layer_out, share_out, share_in, matrix, share_send, share_recv, *scratch):
    rows, width = state.shape
    slots = back.shape[0] // RING // RING
    tp, ep = lax.axis_index("tp"), lax.axis_index("ep")
    y, x = ep // RING, ep % RING
    z, core, chips, partner, right, left = tp_place()

    def group_of(block):
        return (block // RING - x + 2 + RING) % RING

    target = (x * RING + tp % RING, y * RING + (x - group_of(tp) + RING) % RING)
    from_x = tp // RING
    shift = (from_x - x + RING) % RING
    source = (((from_x + shift + 2) % RING) * RING + tp % RING, y * RING + from_x)
    greet([partner, right, left, target, source])
    place = lax.broadcasted_iota(jnp.int32, (slots, rows), 0).astype(F32)
    for r in range(RING):
        for d in range(RING):
            slot = meta[pl.ds(r * 2 * RING + d, 1)]
            gate = meta[pl.ds(r * 2 * RING + RING + d, 1)]
            matrix[pl.ds((r * RING + PLACE[d]) * slots, slots)] = jnp.where(slot == place, gate, 0.0).astype(BF16)

    def term(block):
        span = pl.ds(pl.multiple_of(group_of(block) * RING * slots, RING * slots), RING * slots)
        return lax.dot_general(
            matrix[span],
            back[span, columns(block % RING, width)],
            (((0,), (0,)), ((), ())),
            preferred_element_type=F32,
        )

    shares = []

    def give(h, span, total):
        share_out[span] = total.astype(BF16)
        copy = remote(share_out.at[span], share_in.at[span], share_send.at[h], share_recv.at[h], target)
        copy.start()
        shares.append((span, copy))

    sum_over_tp(term, give, scratch)
    for span, copy in shares:
        copy.wait()
        layer_out[span] = (share_in[span].astype(F32) + state[span].astype(F32)).astype(BF16)


def mix(meta, back, state):
    rows, width = state.shape
    return pl.pallas_call(
        mix_kernel,
        out_shape=jax.ShapeDtypeStruct((rows, width), BF16),
        in_specs=in_vmem(3),
        out_specs=pl.BlockSpec(memory_space=pltpu.VMEM),
        scratch_shapes=[
            pltpu.VMEM((rows, width), BF16),
            pltpu.VMEM((rows, width), BF16),
            pltpu.VMEM((back.shape[0], rows), BF16),
            pltpu.SemaphoreType.DMA((2,)),
            pltpu.SemaphoreType.DMA((2,)),
        ]
        + sum_scratch(rows, width),
        compiler_params=pltpu.CompilerParams(
            collective_id=1, has_side_effects=True, vmem_limit_bytes=VMEM_BYTES
        ),
        name="mix",
    )(meta, back, state)


def slots_of(expert_ids):
    tp, ep = lax.axis_index("tp"), lax.axis_index("ep")
    rows = expert_ids.shape[0]
    mine = tp * RING + (ep // RING + lax.broadcasted_iota(jnp.int32, (1, RING, 1), 1)) % RING
    hit = jnp.any(expert_ids.T[:, None, :] == mine.reshape(1, RING, 1), axis=0)
    upto = (
        lax.broadcasted_iota(jnp.int32, (rows, rows), 0) <= lax.broadcasted_iota(jnp.int32, (rows, rows), 1)
    ).astype(BF16)
    count = jnp.dot(hit.astype(BF16), upto, preferred_element_type=F32)
    places = jnp.where(hit, count - 1.0, -1.0)
    return jnp.concatenate([places, places], axis=0)


def shards(
    context, out_weight, residual, norm_gain, router_weight, expert_ids, w_gate, w_up, w_down
):
    rows = residual.shape[0]
    capacity = min(rows, 2 * rows * expert_ids.shape[1] // router_weight.shape[0])
    back, meta_all, state = layer(
        context,
        out_weight,
        residual,
        slots_of(expert_ids),
        norm_gain.astype(F32)[None],
        router_weight,
        expert_ids,
        w_gate[0],
        w_up[0],
        w_down[0],
        capacity,
    )
    return mix(meta_all, back, state)


def solution(mesh):
    in_specs = (
        P("ep", "tp"),
        P("tp", None),
        P("ep", "tp"),
        P(),
        P(),
        P("ep", None),
        P(("tp", "ep"), None, None),
        P(("tp", "ep"), None, None),
        P(("tp", "ep"), None, None),
    )
    out_specs = P("ep", "tp")
    return jax.shard_map(shards, mesh=mesh, in_specs=in_specs, out_specs=out_specs, check_vma=False)
```

```python
import functools

import jax
import jax.numpy as jnp
from jax import lax
from jax.experimental import pallas as pl
from jax.experimental.pallas import tpu as pltpu
from jax.sharding import PartitionSpec as P

SPLIT = 4
RING = 4
epsilon = 1e-06
MESH = pl.DeviceIdType.MESH
F32 = jnp.float32
BF16 = jnp.bfloat16
VMEM_BYTES = 58 * 2**20
PLACE = (3, 0, 2, 1)
STAGES = ((1, 3), (2,), (0,))
ORDER = (0, 1, 7, 2, 6, 3, 5, 4)
GROUPS = ((0, 1, 2), (3, 4), (5, 6, 7))
DISTANCES = (4, 3, 5, 2, 6, 1, 7, 0)


def in_vmem(count):
    return [pl.BlockSpec(memory_space=pltpu.VMEM)] * count


def columns(index, width):
    return pl.ds(pl.multiple_of(index * width, width), width)


def greet(devices):
    barrier = pltpu.get_barrier_semaphore()
    for device in devices:
        pl.semaphore_signal(barrier, inc=1, device_id=device, device_id_type=MESH)
    pl.semaphore_wait(barrier, len(devices))


def remote(source, target, send, recv, device):
    return pltpu.make_async_remote_copy(
        src_ref=source, dst_ref=target, send_sem=send, recv_sem=recv, device_id=device, device_id_type=MESH
    )


def tp_place():
    tp, ep = lax.axis_index("tp"), lax.axis_index("ep")
    chips = lax.axis_size("tp") // 2
    z, core = tp // 2, tp % 2
    partner = (z * 2 + 1 - core, ep)
    right = (((z + 1) % chips) * 2 + core, ep)
    left = (((z + chips - 1) % chips) * 2 + core, ep)
    return z, core, chips, partner, right, left


def sum_scratch(rows, width):
    block = (rows, width)
    return [
        pltpu.VMEM((8, *block), BF16),
        pltpu.VMEM((8, *block), BF16),
        pltpu.VMEM((8, *block), F32),
        pltpu.VMEM((2, 4, *block), BF16),
        pltpu.VMEM((2, 4, *block), BF16),
        pltpu.SemaphoreType.DMA((8,)),
        pltpu.SemaphoreType.DMA((8,)),
        pltpu.SemaphoreType.DMA((2, 4, 2)),
        pltpu.SemaphoreType.DMA((2, 4, 2)),
    ]


def sum_over_tp(term, give, scratch):
    swap_out, swap_in, pairs, arm_out, arm_in, swap_send, swap_recv, arm_send, arm_recv = scratch
    z, core, chips, partner, right, left = tp_place()
    half = swap_out.shape[1] // 2
    spans = (pl.ds(0, half), pl.ds(half, half))
    swaps = {}
    for j in DISTANCES:
        swap_out[j] = term(((z + j) % chips) * 2 + 1 - core).astype(BF16)
        swaps[j] = remote(swap_out.at[j], swap_in.at[j], swap_send.at[j], swap_recv.at[j], partner)
        swaps[j].start()

    def pair(j):
        mine = term(((z + j) % chips) * 2 + core)
        swaps[j].wait_recv()
        pairs[j] = mine + swap_in[j].astype(F32)

    hops = {}

    def hop(arm, h, step):
        value = pairs[4 - step if arm == 0 else 4 + step, spans[h]]
        if (arm, h, step - 1) in hops:
            hops[arm, h, step - 1].wait_recv()
            value = value + arm_in[arm, step - 1, spans[h]].astype(F32)
        arm_out[arm, step, spans[h]] = value.astype(BF16)
        copy = remote(
            arm_out.at[arm, step, spans[h]],
            arm_in.at[arm, step, spans[h]],
            arm_send.at[arm, step, h],
            arm_recv.at[arm, step, h],
            (right, left)[arm],
        )
        copy.start()
        hops[arm, h, step] = copy

    pair(4)
    hop(0, 0, 0)
    hop(1, 1, 0)
    for step in range(1, 4):
        pair(4 - step)
        pair(4 + step)
        hop(0, 1, step)
        hop(1, 0, step)
        hop(0, 0, step)
        hop(1, 1, step)
    pair(0)
    for h in range(2):
        total = pairs[0, spans[h]]
        for arm in (1 - h, h):
            hops[arm, h, 3].wait_recv()
            total = total + arm_in[arm, 3, spans[h]].astype(F32)
        give(h, spans[h], total)
    for copy in list(hops.values()) + list(swaps.values()):
        copy.wait_send()


class GatherOverTp:
    def __init__(self, out, width, sems):
        self.out, self.width = out, width
        self.arm_send, self.arm_recv, self.near_send, self.near_recv = sems
        z, self.core, chips, self.partner, self.right, self.left = tp_place()
        self.half = out.shape[0] // 2
        self.copies = []

    def at(self, j, h, side):
        offset = pl.multiple_of((ORDER.index(j % 8) * 2 + side) * self.width, self.width)
        return self.out.at[pl.ds(h * self.half, self.half), pl.ds(offset, self.width)]

    def go(self, source, target, send, recv, device):
        copy = remote(source, target, send, recv, device)
        copy.start()
        self.copies.append(copy)

    def pass_on(self, arm, h, step):
        sign = 1 if arm else -1
        self.go(
            self.at(sign * step, h, self.core),
            self.at(sign * (step + 1), h, self.core),
            self.arm_send.at[arm, step, h],
            self.arm_recv.at[arm, step, h],
            (self.right, self.left)[arm],
        )

    def to_partner(self, j, h):
        ref = self.at(j, h, self.core)
        self.go(ref, ref, self.near_send.at[j % 8, h], self.near_recv.at[j % 8, h], self.partner)

    def start(self, h):
        for arm in (h, 1 - h):
            self.pass_on(arm, h, 0)
        self.to_partner(0, h)

    def step(self, step):
        for arm, h in ((0, 0), (1, 0), (1, 1), (0, 1)):
            if step == 4 and arm != h:
                continue
            j = step if arm else -step
            ref = self.at(j, h, self.core)
            remote(
                ref, ref, self.arm_send.at[arm, step - 1, h], self.arm_recv.at[arm, step - 1, h], self.right
            ).wait_recv()
            if step < 3 or (step == 3 and arm == h):
                self.pass_on(arm, h, step)
            self.to_partner(j, h)

    def ready(self, j):
        for h in range(2):
            ref = self.at(j, h, 1 - self.core)
            remote(ref, ref, self.near_send.at[j % 8, h], self.near_recv.at[j % 8, h], self.partner).wait_recv()

    def finish(self):
        for copy in self.copies:
            copy.wait_send()


def layer_kernel(
    context, weight, residual, places, gain, router, ids, gate, up, down,
    share_in, state,
    back, meta_all, matrix, share_out, hidden, squares, selector, packed, meta, rows, gate_up, spread, inner, out, *scratch
):
    total_scratch, gather_sems, (spread_send, spread_recv) = scratch[:9], scratch[9:13], scratch[13:15]
    (load, y_send, y_recv, right_send, right_recv, left_send, left_recv, far_send, far_recv, meta_send, meta_recv,
     in_send, in_recv, on_send, on_recv, out_send, out_recv, share_send, share_recv) = scratch[15:34]
    last_scratch = scratch[34:]
    tp, ep = lax.axis_index("tp"), lax.axis_index("ep")
    y, x = ep // RING, ep % RING
    z, core, chips, partner, z_right, z_left = tp_place()
    tokens, share = residual.shape
    slots = packed.shape[0] // RING
    width = weight.shape[1]
    block = RING * slots
    hidden_units = gate.shape[1]
    pieces = hidden_units // 128
    quarter = width // RING
    pair = 2 * share

    def device(dy, dx):
        return (tp, ((y + dy + RING) % RING) * RING + (x + dx + RING) % RING)

    right, left = device(0, 1), device(0, -1)

    def group_of(index):
        return (index // RING - x + 2 + RING) % RING

    owner = (x * RING + tp % RING, y * RING + (x - group_of(tp) + RING) % RING)
    from_x = tp // RING
    origin = ((2 * from_x - x + 2 + RING) % RING * RING + tp % RING, y * RING + from_x)
    greet(
        [partner, z_right, z_left, owner, origin]
        + [device(0, k) for k in range(1, RING)]
        + [device(k, 0) for k in range(1, RING)]
    )

    def chunk(r, d):
        return pl.ds(r * block + PLACE[d] * slots, slots)

    def unit_span(r, h):
        return pl.ds(r * block + PLACE[STAGES[h][0]] * slots, len(STAGES[h]) * slots)

    def half_span(r, h, side):
        half = len(STAGES[h]) * slots // 2
        return pl.ds(r * block + PLACE[STAGES[h][0]] * slots + side * half, half)

    def inner_columns(k):
        return pl.ds(k * hidden_units, hidden_units)

    copies = []

    def send(source, target, send_sem, recv_sem, to):
        copy = remote(source, target, send_sem, recv_sem, to)
        copy.start()
        copies.append(copy)
        return copy

    spreads = [
        send(
            down.at[:, columns((x + k) % RING, quarter)],
            spread.at[pl.ds(k * hidden_units, hidden_units)],
            spread_send.at[k],
            spread_recv.at[k],
            device(0, k),
        )
        for k in range(1, RING)
    ]
    loads = [(down.at[:, columns(x, quarter)], spread.at[pl.ds(0, hidden_units)])]
    for p, j in enumerate(ORDER):
        source = pl.ds(pl.multiple_of((z + j) % chips * pair, pair), pair)
        target = pl.ds(p * pair, pair)
        for i in range(pieces):
            part = pl.ds(i * 128, 128)
            loads.append((gate.at[source, part], gate_up.at[target, pl.ds(i * 256, 128)]))
            loads.append((up.at[source, part], gate_up.at[target, pl.ds(i * 256 + 128, 128)]))
    loads = [pltpu.make_async_copy(a, b, load.at[i]) for i, (a, b) in enumerate(loads)]
    for copy in loads:
        copy.start()
    place = lax.broadcasted_iota(jnp.int32, (slots, tokens), 0).astype(F32)
    for d in range(RING):
        selector[pl.ds(PLACE[d] * slots, slots)] = jnp.where(places[pl.ds(d, 1)] == place, 1.0, 0.0).astype(BF16)
    squares[...] = jnp.zeros_like(squares)
    gather = GatherOverTp(hidden, share, gather_sems)

    def term(index):
        return jnp.dot(context[...], weight[:, columns(index, share)], preferred_element_type=F32)

    def give(h, span, total):
        mine = (total + residual[span].astype(F32)).astype(BF16)
        state[span] = mine
        hidden[span, columns(core, share)] = mine
        gather.start(h)

    sum_over_tp(term, give, total_scratch)
    y_copies, sides = {}, {}

    def group_columns(g):
        first, last = GROUPS[g][0], GROUPS[g][-1] + 1
        return pl.ds(first * pair, (last - first) * pair + (128 if g == len(GROUPS) - 1 else 0))

    def to_sides(d, g, source):
        part = group_columns(g)
        sides[d, g] = (
            send(source, rows.at[chunk(1, d), part], right_send.at[d, g], right_recv.at[d, g], right),
            send(source, rows.at[chunk(3, d), part], left_send.at[d, g], left_recv.at[d, g], left),
        )

    def y_arrived(d, g):
        y_copies[d, g].wait_recv()
        to_sides(d, g, rows.at[chunk(0, d), group_columns(g)])

    def gain_of(index):
        lines = pair // 128
        return jnp.concatenate([gain[pl.ds(index * lines + i, 1)] for i in range(lines)], axis=1)

    def dispatch(g):
        for p in GROUPS[g]:
            gather.ready(ORDER[p])
            part = pl.ds(p * pair, pair)
            value = hidden[:, part].astype(F32)
            total = squares[...]
            for i in range(pair // 128):
                lanes = value[:, i * 128 : (i + 1) * 128]
                total = total + lanes * lanes
            squares[...] = total
            scaled = (value * gain_of((z + ORDER[p]) % chips)).astype(BF16)
            packed[:, part] = jnp.dot(selector[...], scaled, preferred_element_type=F32).astype(BF16)
        if g == len(GROUPS) - 1:
            mean = jnp.sum(squares[...], axis=1, keepdims=True) / width
            inverse = lax.rsqrt(mean + epsilon)
            high = inverse.astype(BF16).astype(F32)
            lane = lax.broadcasted_iota(jnp.int32, (tokens, 128), 1)
            parts = jnp.where(lane == 0, high, jnp.where(lane == 1, inverse - high, 0.0)).astype(BF16)
            packed[:, pl.ds(width, 128)] = jnp.dot(selector[...], parts, preferred_element_type=F32).astype(BF16)
        part = group_columns(g)
        for d in (1, 3, 2):
            y_copies[d, g] = send(
                packed.at[chunk(0, d), part], rows.at[chunk(0, d), part], y_send.at[d, g], y_recv.at[d, g], device(d, 0)
            )
        to_sides(0, g, packed.at[chunk(0, 0), part])
        rows[chunk(0, 0), part] = packed[chunk(0, 0), part]

    def unit(r, h):
        span = unit_span(r, h)
        parts = rows[span, pl.ds(width, 128)].astype(F32)
        inverse = parts[:, 0:1] + parts[:, 1:2]

        def step(j, carry):
            both = jnp.dot(rows[span, pl.ds(0, width)], gate_up[:, columns(j, 256)], preferred_element_type=F32)
            both = both * inverse
            value, scale = both[:, :128], both[:, 128:]
            inner[span, columns(j, 128)] = (value / (1.0 + jnp.exp(-value)) * scale).astype(BF16)
            return carry

        lax.fori_loop(0, pieces, step, 0)
        for k in (1, 3):
            there = (r + k) % RING
            send(
                inner.at[span, inner_columns(0)],
                inner.at[unit_span(there, h), inner_columns(k)],
                in_send.at[r, h, k],
                in_recv.at[there, h, k],
                device(0, k),
            )

    def relay(r, h):
        for side, k in ((0, 1), (1, 3)):
            here, there = (r + k) % RING, (r + 2) % RING
            ref = inner.at[unit_span(here, h), inner_columns(k)]
            remote(ref, ref, in_send.at[r, h, k], in_recv.at[here, h, k], right).wait_recv()
            send(
                inner.at[half_span(here, h, side), inner_columns(k)],
                inner.at[half_span(there, h, side), inner_columns(2)],
                on_send.at[r, h, side],
                on_recv.at[there, h, side],
                (right, left)[side],
            )

    def came_right(d):
        for g in range(len(GROUPS)):
            sides[d, g][0].wait_recv()

    def came_left(d):
        for g in range(len(GROUPS)):
            sides[d, g][1].wait_recv()

    far = {}

    def onward(h, side):
        far[h, side] = send(
            rows.at[half_span((1, 3)[side], h, side)],
            rows.at[half_span(2, h, side)],
            far_send.at[h, side],
            far_recv.at[h, side],
            (right, left)[side],
        )

    def came_far(h):
        far[h, 0].wait_recv()
        far[h, 1].wait_recv()

    def finish(r, h):
        span = unit_span(r, h)
        for side in range(2):
            ref = inner.at[half_span(r, h, side), inner_columns(2)]
            remote(ref, ref, on_send.at[r, h, side], on_recv.at[r, h, side], right).wait_recv()

        def step(n, carry):
            out[span, columns(n, 256)] = jnp.dot(
                inner[span], spread[:, columns(n, 256)], preferred_element_type=F32
            ).astype(BF16)
            return carry

        lax.fori_loop(0, quarter // 256, step, 0)
        for d in STAGES[h]:
            target = back.at[chunk(r, d)]
            if d == 0:
                copy = pltpu.make_async_copy(out.at[chunk(r, 0)], target, out_send.at[r, 0])
                copy.start()
                kept.append(copy)
            else:
                send(out.at[chunk(r, d)], target, out_send.at[r, d], out_recv.at[r, d], device(-d, 0))

    def gates():
        inverse = lax.rsqrt(jnp.sum(squares[...], axis=1, keepdims=True) / width + epsilon)
        count = router.shape[0]
        logits = jnp.zeros((count, tokens), F32)
        for p, j in enumerate(ORDER):
            index = (z + j) % chips
            normed = (hidden[:, pl.ds(p * pair, pair)].astype(F32) * inverse * gain_of(index)).astype(BF16)
            logits = logits + lax.dot_general(
                router[:, columns(index, pair)], normed, (((1,), (1,)), ((), ())), preferred_element_type=F32
            )
        every = lax.broadcasted_iota(jnp.int32, (count, tokens), 0)
        hit = every == ids[0:1]
        for k in range(1, ids.shape[0]):
            hit = hit | (every == ids[k : k + 1])
        top = jnp.max(jnp.where(hit, logits, -jnp.inf), axis=0, keepdims=True)
        raised = jnp.where(hit, jnp.exp(jnp.where(hit, logits - top, 0.0)), 0.0)
        softmax = raised / jnp.sum(raised, axis=0, keepdims=True)
        for d in range(RING):
            own = every == tp * RING + (y + d) % RING
            meta[pl.ds(RING + d, 1)] = jnp.sum(jnp.where(own, softmax, 0.0), axis=0, keepdims=True)
        meta[pl.ds(0, RING)] = places[pl.ds(0, RING)]

    gather.step(1)
    dispatch(0)
    gather.step(2)
    dispatch(1)
    y_arrived(1, 0)
    y_arrived(3, 0)
    gather.step(3)
    gather.step(4)
    dispatch(2)
    y_arrived(1, 1)
    y_arrived(3, 1)
    gates()
    meta_all[pl.ds(0, 2 * RING)] = meta[...]
    metas = [
        send(meta, meta_all.at[pl.ds(k * 2 * RING, 2 * RING)], meta_send.at[k], meta_recv.at[k], device(0, k))
        for k in range(1, RING)
    ]
    y_arrived(1, 2)
    y_arrived(3, 2)
    for copy in loads:
        copy.wait()
    kept = []
    unit(0, 0)
    came_right(0)
    came_left(0)
    unit(0, 2)
    for g in range(3):
        y_arrived(2, g)
    came_right(1)
    onward(0, 0)
    came_left(3)
    onward(0, 1)
    came_left(1)
    came_right(3)
    unit(1, 0)
    unit(3, 0)
    relay(0, 0)
    unit(1, 2)
    unit(3, 2)
    unit(0, 1)
    came_right(2)
    onward(1, 0)
    came_left(2)
    onward(1, 1)
    onward(2, 0)
    onward(2, 1)
    relay(1, 0)
    relay(3, 0)
    came_far(0)
    unit(2, 0)
    unit(1, 1)
    unit(3, 1)
    relay(0, 1)
    relay(0, 2)
    relay(2, 0)
    for copy in spreads:
        copy.wait_recv()
    for r in (0, 1, 3, 2):
        finish(r, 0)
    relay(1, 1)
    relay(3, 1)
    came_far(1)
    unit(2, 1)
    relay(1, 2)
    relay(3, 2)
    came_far(2)
    unit(2, 2)
    relay(2, 1)
    for r in (0, 1, 3, 2):
        finish(r, 1)
    relay(2, 2)
    for r in (0, 1, 3, 2):
        finish(r, 2)
    for copy in kept:
        copy.wait()
    for r in range(RING):
        for d in range(1, RING):
            ref = back.at[chunk(r, d)]
            remote(ref, ref, out_send.at[r, d], out_recv.at[r, d], device(d, 0)).wait_recv()
    for copy in metas:
        copy.wait_recv()
    for r in range(RING):
        for d in range(RING):
            slot = meta_all[pl.ds(r * 2 * RING + d, 1)]
            value = meta_all[pl.ds(r * 2 * RING + RING + d, 1)]
            matrix[pl.ds((r * RING + PLACE[d]) * slots, slots)] = jnp.where(slot == place, value, 0.0).astype(BF16)

    def mixed(index):
        span = pl.ds(pl.multiple_of(group_of(index) * block, block), block)
        return lax.dot_general(
            matrix[span],
            back[span, columns(index % RING, share)],
            (((0,), (0,)), ((), ())),
            preferred_element_type=F32,
        )

    def deliver(h, span, total):
        share_out[span] = total.astype(BF16)
        shares.append(
            send(share_out.at[span], share_in.at[span], share_send.at[h], share_recv.at[h], owner)
        )

    shares = []
    sum_over_tp(mixed, deliver, last_scratch)
    for copy in shares:
        copy.wait_recv()
    gather.finish()
    for copy in copies:
        copy.wait_send()


def layer(context, weight, residual, places, gain, router, ids, gate, up, down, slots):
    tokens, share = residual.shape
    width, hidden_units = gate.shape
    total = RING * slots
    dma = pltpu.SemaphoreType.DMA
    return pl.pallas_call(
        layer_kernel,
        out_shape=(
            jax.ShapeDtypeStruct((tokens, share), BF16),
            jax.ShapeDtypeStruct((tokens, share), BF16),
        ),
        in_specs=in_vmem(7) + [pl.BlockSpec(memory_space=pl.ANY)] * 3,
        out_specs=tuple(in_vmem(2)),
        scratch_shapes=[
            pltpu.VMEM((RING * total, width // RING), BF16),
            pltpu.VMEM((RING * 2 * RING, tokens), F32),
            pltpu.VMEM((RING * total, tokens), BF16),
            pltpu.VMEM((tokens, share), BF16),
            pltpu.VMEM((tokens, width), BF16),
            pltpu.VMEM((tokens, 128), F32),
            pltpu.VMEM((total, tokens), BF16),
            pltpu.VMEM((total, width + 128), BF16),
            pltpu.VMEM((2 * RING, tokens), F32),
            pltpu.VMEM((RING * total, width + 128), BF16),
            pltpu.VMEM((width, 2 * hidden_units), BF16),
            pltpu.VMEM((RING * hidden_units, width // RING), BF16),
            pltpu.VMEM((RING * total, RING * hidden_units), BF16),
            pltpu.VMEM((RING * total, width // RING), BF16),
        ]
        + sum_scratch(tokens, share)
        + [dma((2, 4, 2))] * 2
        + [dma((8, 2))] * 2
        + [dma((RING,))] * 2
        + [dma((hidden_units // 128 * 16 + 1,))]
        + [dma((RING, 3))] * 6
        + [dma((3, 2))] * 2
        + [dma((RING,))] * 2
        + [dma((RING, 3, RING))] * 2
        + [dma((RING, 3, 2))] * 2
        + [dma((RING, RING))] * 2
        + [dma((2,))] * 2
        + sum_scratch(tokens, share),
        compiler_params=pltpu.CompilerParams(
            collective_id=0, has_side_effects=True, vmem_limit_bytes=VMEM_BYTES
        ),
        name="layer",
    )(context, weight, residual, places, gain, router, ids, gate, up, down)


def slots_of(expert_ids):
    tp, ep = lax.axis_index("tp"), lax.axis_index("ep")
    rows = expert_ids.shape[0]
    mine = tp * RING + (ep // RING + lax.broadcasted_iota(jnp.int32, (1, RING, 1), 1)) % RING
    hit = jnp.any(expert_ids.T[:, None, :] == mine.reshape(1, RING, 1), axis=0)
    upto = (
        lax.broadcasted_iota(jnp.int32, (rows, rows), 0) <= lax.broadcasted_iota(jnp.int32, (rows, rows), 1)
    ).astype(BF16)
    count = jnp.dot(hit.astype(BF16), upto, preferred_element_type=F32)
    places = jnp.where(hit, count - 1.0, -1.0)
    return jnp.concatenate([places, places], axis=0)


def shards(
    context, out_weight, residual, norm_gain, router_weight, expert_ids, w_gate, w_up, w_down
):
    rows = residual.shape[0]
    capacity = min(rows, 2 * rows * expert_ids.shape[1] // router_weight.shape[0])
    share, state = layer(
        context,
        out_weight,
        residual,
        slots_of(expert_ids),
        norm_gain.astype(F32).reshape(-1, 128),
        router_weight,
        expert_ids.T,
        w_gate[0],
        w_up[0],
        w_down[0],
        capacity,
    )
    return (share.astype(F32) + state.astype(F32)).astype(BF16)


def solution(mesh):
    in_specs = (
        P("ep", "tp"),
        P("tp", None),
        P("ep", "tp"),
        P(),
        P(),
        P("ep", None),
        P(("tp", "ep"), None, None),
        P(("tp", "ep"), None, None),
        P(("tp", "ep"), None, None),
    )
    out_specs = P("ep", "tp")
    return jax.shard_map(shards, mesh=mesh, in_specs=in_specs, out_specs=out_specs, check_vma=False)
```

```python
import functools

import jax
import jax.numpy as jnp
from jax import lax
from jax.experimental import pallas as pl
from jax.experimental.pallas import tpu as pltpu
from jax.sharding import PartitionSpec as P

SPLIT = 4
RING = 4
epsilon = 1e-06
MESH = pl.DeviceIdType.MESH
F32 = jnp.float32
BF16 = jnp.bfloat16
VMEM_BYTES = 58 * 2**20
PLACE = (3, 0, 2, 1)
STAGES = ((1, 3), (2,), (0,))
ORDER = (0, 1, 7, 2, 6, 3, 5, 4)
GROUPS = ((0, 1, 2), (3, 4), (5, 6, 7))
DISTANCES = (4, 3, 5, 2, 6, 1, 7, 0)


def in_vmem(count):
    return [pl.BlockSpec(memory_space=pltpu.VMEM)] * count


def columns(index, width):
    return pl.ds(pl.multiple_of(index * width, width), width)


def greet(devices):
    barrier = pltpu.get_barrier_semaphore()
    for device in devices:
        pl.semaphore_signal(barrier, inc=1, device_id=device, device_id_type=MESH)
    pl.semaphore_wait(barrier, len(devices))


def remote(source, target, send, recv, device):
    return pltpu.make_async_remote_copy(
        src_ref=source, dst_ref=target, send_sem=send, recv_sem=recv, device_id=device, device_id_type=MESH
    )


def tp_place():
    tp, ep = lax.axis_index("tp"), lax.axis_index("ep")
    chips = lax.axis_size("tp") // 2
    z, core = tp // 2, tp % 2
    partner = (z * 2 + 1 - core, ep)
    right = (((z + 1) % chips) * 2 + core, ep)
    left = (((z + chips - 1) % chips) * 2 + core, ep)
    return z, core, chips, partner, right, left


def sum_scratch(rows, width):
    block = (rows, width)
    return [
        pltpu.VMEM((8, *block), BF16),
        pltpu.VMEM((8, *block), BF16),
        pltpu.VMEM((8, *block), F32),
        pltpu.VMEM((2, 4, *block), BF16),
        pltpu.VMEM((2, 4, *block), BF16),
        pltpu.SemaphoreType.DMA((8,)),
        pltpu.SemaphoreType.DMA((8,)),
        pltpu.SemaphoreType.DMA((2, 4, 2)),
        pltpu.SemaphoreType.DMA((2, 4, 2)),
    ]


def sum_over_tp(term, give, scratch):
    swap_out, swap_in, pairs, arm_out, arm_in, swap_send, swap_recv, arm_send, arm_recv = scratch
    z, core, chips, partner, right, left = tp_place()
    half = swap_out.shape[1] // 2
    spans = (pl.ds(0, half), pl.ds(half, half))
    swaps = {}
    for j in DISTANCES:
        swap_out[j] = term(((z + j) % chips) * 2 + 1 - core).astype(BF16)
        swaps[j] = remote(swap_out.at[j], swap_in.at[j], swap_send.at[j], swap_recv.at[j], partner)
        swaps[j].start()

    def pair(j):
        mine = term(((z + j) % chips) * 2 + core)
        swaps[j].wait_recv()
        pairs[j] = mine + swap_in[j].astype(F32)

    hops = {}

    def hop(arm, h, step):
        value = pairs[4 - step if arm == 0 else 4 + step, spans[h]]
        if (arm, h, step - 1) in hops:
            hops[arm, h, step - 1].wait_recv()
            value = value + arm_in[arm, step - 1, spans[h]].astype(F32)
        arm_out[arm, step, spans[h]] = value.astype(BF16)
        copy = remote(
            arm_out.at[arm, step, spans[h]],
            arm_in.at[arm, step, spans[h]],
            arm_send.at[arm, step, h],
            arm_recv.at[arm, step, h],
            (right, left)[arm],
        )
        copy.start()
        hops[arm, h, step] = copy

    pair(4)
    hop(0, 0, 0)
    hop(1, 1, 0)
    for step in range(1, 4):
        pair(4 - step)
        pair(4 + step)
        hop(0, 1, step)
        hop(1, 0, step)
        hop(0, 0, step)
        hop(1, 1, step)
    pair(0)
    for h in range(2):
        total = pairs[0, spans[h]]
        for arm in (1 - h, h):
            hops[arm, h, 3].wait_recv()
            total = total + arm_in[arm, 3, spans[h]].astype(F32)
        give(h, spans[h], total)
    for copy in list(hops.values()) + list(swaps.values()):
        copy.wait_send()


class GatherOverTp:
    def __init__(self, out, width, sems):
        self.out, self.width = out, width
        self.arm_send, self.arm_recv, self.near_send, self.near_recv = sems
        z, self.core, chips, self.partner, self.right, self.left = tp_place()
        self.half = out.shape[0] // 2
        self.copies = []

    def at(self, j, h, side):
        offset = pl.multiple_of((ORDER.index(j % 8) * 2 + side) * self.width, self.width)
        return self.out.at[pl.ds(h * self.half, self.half), pl.ds(offset, self.width)]

    def go(self, source, target, send, recv, device):
        copy = remote(source, target, send, recv, device)
        copy.start()
        self.copies.append(copy)

    def pass_on(self, arm, h, step):
        sign = 1 if arm else -1
        self.go(
            self.at(sign * step, h, self.core),
            self.at(sign * (step + 1), h, self.core),
            self.arm_send.at[arm, step, h],
            self.arm_recv.at[arm, step, h],
            (self.right, self.left)[arm],
        )

    def to_partner(self, j, h):
        ref = self.at(j, h, self.core)
        self.go(ref, ref, self.near_send.at[j % 8, h], self.near_recv.at[j % 8, h], self.partner)

    def start(self, h):
        for arm in (h, 1 - h):
            self.pass_on(arm, h, 0)
        self.to_partner(0, h)

    def step(self, step):
        for arm, h in ((0, 0), (1, 0), (1, 1), (0, 1)):
            if step == 4 and arm != h:
                continue
            j = step if arm else -step
            ref = self.at(j, h, self.core)
            remote(
                ref, ref, self.arm_send.at[arm, step - 1, h], self.arm_recv.at[arm, step - 1, h], self.right
            ).wait_recv()
            if step < 3 or (step == 3 and arm == h):
                self.pass_on(arm, h, step)
            self.to_partner(j, h)

    def ready(self, j):
        for h in range(2):
            ref = self.at(j, h, 1 - self.core)
            remote(ref, ref, self.near_send.at[j % 8, h], self.near_recv.at[j % 8, h], self.partner).wait_recv()

    def finish(self):
        for copy in self.copies:
            copy.wait_send()


def layer_kernel(
    context, weight, residual, places, gain, router, ids, gate, up, down,
    share_in, state,
    back, meta_all, matrix, share_out, hidden, squares, selector, packed, meta, rows, gate_up, spread, inner, out, *scratch
):
    total_scratch, gather_sems, (spread_send, spread_recv) = scratch[:9], scratch[9:13], scratch[13:15]
    (load, y_send, y_recv, right_send, right_recv, left_send, left_recv, far_send, far_recv, meta_send, meta_recv,
     in_send, in_recv, on_send, on_recv, out_send, out_recv, share_send, share_recv) = scratch[15:34]
    last_scratch = scratch[34:]
    tp, ep = lax.axis_index("tp"), lax.axis_index("ep")
    y, x = ep // RING, ep % RING
    z, core, chips, partner, z_right, z_left = tp_place()
    tokens, share = residual.shape
    slots = packed.shape[0] // RING
    width = weight.shape[1]
    block = RING * slots
    hidden_units = gate.shape[1]
    pieces = hidden_units // 128
    quarter = width // RING
    pair = 2 * share

    def device(dy, dx):
        return (tp, ((y + dy + RING) % RING) * RING + (x + dx + RING) % RING)

    right, left = device(0, 1), device(0, -1)

    def group_of(index):
        return (index // RING - x + 2 + RING) % RING

    owner = (x * RING + tp % RING, y * RING + (x - group_of(tp) + RING) % RING)
    from_x = tp // RING
    origin = ((2 * from_x - x + 2 + RING) % RING * RING + tp % RING, y * RING + from_x)
    greet(
        [partner, z_right, z_left, owner, origin]
        + [device(0, k) for k in range(1, RING)]
        + [device(k, 0) for k in range(1, RING)]
    )

    def chunk(r, d):
        return pl.ds(r * block + PLACE[d] * slots, slots)

    def unit_span(r, h):
        return pl.ds(r * block + PLACE[STAGES[h][0]] * slots, len(STAGES[h]) * slots)

    def half_span(r, h, side):
        half = len(STAGES[h]) * slots // 2
        return pl.ds(r * block + PLACE[STAGES[h][0]] * slots + side * half, half)

    def inner_columns(k):
        return pl.ds(k * hidden_units, hidden_units)

    copies = []

    def send(source, target, send_sem, recv_sem, to):
        copy = remote(source, target, send_sem, recv_sem, to)
        copy.start()
        copies.append(copy)
        return copy

    spreads = [
        send(
            down.at[:, columns((x + k) % RING, quarter)],
            spread.at[pl.ds(k * hidden_units, hidden_units)],
            spread_send.at[k],
            spread_recv.at[k],
            device(0, k),
        )
        for k in range(1, RING)
    ]
    loads = [(down.at[:, columns(x, quarter)], spread.at[pl.ds(0, hidden_units)])]
    for p, j in enumerate(ORDER):
        source = pl.ds(pl.multiple_of((z + j) % chips * pair, pair), pair)
        target = pl.ds(p * pair, pair)
        for i in range(pieces):
            part = pl.ds(i * 128, 128)
            loads.append((gate.at[source, part], gate_up.at[target, pl.ds(i * 256, 128)]))
            loads.append((up.at[source, part], gate_up.at[target, pl.ds(i * 256 + 128, 128)]))
    loads = [pltpu.make_async_copy(a, b, load.at[i]) for i, (a, b) in enumerate(loads)]
    for copy in loads:
        copy.start()
    place = lax.broadcasted_iota(jnp.int32, (slots, tokens), 0).astype(F32)
    for d in range(RING):
        selector[pl.ds(PLACE[d] * slots, slots)] = jnp.where(places[pl.ds(d, 1)] == place, 1.0, 0.0).astype(BF16)
    squares[...] = jnp.zeros_like(squares)
    gather = GatherOverTp(hidden, share, gather_sems)

    def term(index):
        return jnp.dot(context[...], weight[:, columns(index, share)], preferred_element_type=F32)

    def give(h, span, total):
        mine = (total + residual[span].astype(F32)).astype(BF16)
        state[span] = mine
        hidden[span, columns(core, share)] = mine
        gather.start(h)

    sum_over_tp(term, give, total_scratch)
    y_copies, sides = {}, {}

    def group_columns(g):
        first, last = GROUPS[g][0], GROUPS[g][-1] + 1
        return pl.ds(first * pair, (last - first) * pair + (128 if g == len(GROUPS) - 1 else 0))

    def to_sides(d, g, source):
        part = group_columns(g)
        sides[d, g] = (
            send(source, rows.at[chunk(1, d), part], right_send.at[d, g], right_recv.at[d, g], right),
            send(source, rows.at[chunk(3, d), part], left_send.at[d, g], left_recv.at[d, g], left),
        )

    def y_arrived(d, g):
        y_copies[d, g].wait_recv()
        to_sides(d, g, rows.at[chunk(0, d), group_columns(g)])

    def gain_of(index):
        lines = pair // 128
        return jnp.concatenate([gain[pl.ds(index * lines + i, 1)] for i in range(lines)], axis=1)

    def dispatch(g):
        for p in GROUPS[g]:
            gather.ready(ORDER[p])
            part = pl.ds(p * pair, pair)
            value = hidden[:, part].astype(F32)
            total = squares[...]
            for i in range(pair // 128):
                lanes = value[:, i * 128 : (i + 1) * 128]
                total = total + lanes * lanes
            squares[...] = total
            scaled = (value * gain_of((z + ORDER[p]) % chips)).astype(BF16)
            packed[:, part] = jnp.dot(selector[...], scaled, preferred_element_type=F32).astype(BF16)
        if g == len(GROUPS) - 1:
            mean = jnp.sum(squares[...], axis=1, keepdims=True) / width
            inverse = lax.rsqrt(mean + epsilon)
            high = inverse.astype(BF16).astype(F32)
            lane = lax.broadcasted_iota(jnp.int32, (tokens, 128), 1)
            parts = jnp.where(lane == 0, high, jnp.where(lane == 1, inverse - high, 0.0)).astype(BF16)
            packed[:, pl.ds(width, 128)] = jnp.dot(selector[...], parts, preferred_element_type=F32).astype(BF16)
        part = group_columns(g)
        for d in (1, 3, 2):
            y_copies[d, g] = send(
                packed.at[chunk(0, d), part], rows.at[chunk(0, d), part], y_send.at[d, g], y_recv.at[d, g], device(d, 0)
            )
        to_sides(0, g, packed.at[chunk(0, 0), part])
        rows[chunk(0, 0), part] = packed[chunk(0, 0), part]

    def unit(r, h):
        span = unit_span(r, h)
        parts = rows[span, pl.ds(width, 128)].astype(F32)
        inverse = parts[:, 0:1] + parts[:, 1:2]

        def step(j, carry):
            both = jnp.dot(rows[span, pl.ds(0, width)], gate_up[:, columns(j, 256)], preferred_element_type=F32)
            both = both * inverse
            value, scale = both[:, :128], both[:, 128:]
            inner[span, columns(j, 128)] = (value / (1.0 + jnp.exp(-value)) * scale).astype(BF16)
            return carry

        lax.fori_loop(0, pieces, step, 0)
        for k in (1, 3):
            there = (r + k) % RING
            send(
                inner.at[span, inner_columns(0)],
                inner.at[unit_span(there, h), inner_columns(k)],
                in_send.at[r, h, k],
                in_recv.at[there, h, k],
                device(0, k),
            )

    def relay(r, h):
        for side, k in ((0, 1), (1, 3)):
            here, there = (r + k) % RING, (r + 2) % RING
            ref = inner.at[unit_span(here, h), inner_columns(k)]
            remote(ref, ref, in_send.at[r, h, k], in_recv.at[here, h, k], right).wait_recv()
            send(
                inner.at[half_span(here, h, side), inner_columns(k)],
                inner.at[half_span(there, h, side), inner_columns(2)],
                on_send.at[r, h, side],
                on_recv.at[there, h, side],
                (right, left)[side],
            )

    def came_right(d):
        for g in range(len(GROUPS)):
            sides[d, g][0].wait_recv()

    def came_left(d):
        for g in range(len(GROUPS)):
            sides[d, g][1].wait_recv()

    far = {}

    def onward(h, side):
        far[h, side] = send(
            rows.at[half_span((1, 3)[side], h, side)],
            rows.at[half_span(2, h, side)],
            far_send.at[h, side],
            far_recv.at[h, side],
            (right, left)[side],
        )

    def came_far(h):
        far[h, 0].wait_recv()
        far[h, 1].wait_recv()

    def finish(r, h):
        span = unit_span(r, h)
        for side in range(2):
            ref = inner.at[half_span(r, h, side), inner_columns(2)]
            remote(ref, ref, on_send.at[r, h, side], on_recv.at[r, h, side], right).wait_recv()

        def step(n, carry):
            out[span, columns(n, 256)] = jnp.dot(
                inner[span], spread[:, columns(n, 256)], preferred_element_type=F32
            ).astype(BF16)
            return carry

        lax.fori_loop(0, quarter // 256, step, 0)
        for d in STAGES[h]:
            target = back.at[chunk(r, d)]
            if d == 0:
                copy = pltpu.make_async_copy(out.at[chunk(r, 0)], target, out_send.at[r, 0])
                copy.start()
                kept.append(copy)
            else:
                send(out.at[chunk(r, d)], target, out_send.at[r, d], out_recv.at[r, d], device(-d, 0))

    def gates():
        inverse = lax.rsqrt(jnp.sum(squares[...], axis=1, keepdims=True) / width + epsilon)
        count = router.shape[0]
        logits = jnp.zeros((count, tokens), F32)
        for p, j in enumerate(ORDER):
            index = (z + j) % chips
            normed = (hidden[:, pl.ds(p * pair, pair)].astype(F32) * inverse * gain_of(index)).astype(BF16)
            logits = logits + lax.dot_general(
                router[:, columns(index, pair)], normed, (((1,), (1,)), ((), ())), preferred_element_type=F32
            )
        every = lax.broadcasted_iota(jnp.int32, (count, tokens), 0)
        hit = every == ids[0:1]
        for k in range(1, ids.shape[0]):
            hit = hit | (every == ids[k : k + 1])
        top = jnp.max(jnp.where(hit, logits, -jnp.inf), axis=0, keepdims=True)
        raised = jnp.where(hit, jnp.exp(jnp.where(hit, logits - top, 0.0)), 0.0)
        softmax = raised / jnp.sum(raised, axis=0, keepdims=True)
        for d in range(RING):
            own = every == tp * RING + (y + d) % RING
            meta[pl.ds(RING + d, 1)] = jnp.sum(jnp.where(own, softmax, 0.0), axis=0, keepdims=True)
        meta[pl.ds(0, RING)] = places[pl.ds(0, RING)]

    gather.step(1)
    dispatch(0)
    gather.step(2)
    dispatch(1)
    y_arrived(1, 0)
    y_arrived(3, 0)
    gather.step(3)
    gather.step(4)
    dispatch(2)
    y_arrived(1, 1)
    y_arrived(3, 1)
    gates()
    meta_all[pl.ds(0, 2 * RING)] = meta[...]
    metas = [
        send(meta, meta_all.at[pl.ds(k * 2 * RING, 2 * RING)], meta_send.at[k], meta_recv.at[k], device(0, k))
        for k in range(1, RING)
    ]
    y_arrived(1, 2)
    y_arrived(3, 2)
    for copy in loads:
        copy.wait()
    kept = []
    unit(0, 0)
    came_right(0)
    came_left(0)
    unit(0, 2)
    came_right(1)
    onward(0, 0)
    came_left(3)
    onward(0, 1)
    for g in range(3):
        y_arrived(2, g)
    came_left(1)
    came_right(3)
    unit(1, 0)
    unit(3, 0)
    relay(0, 0)
    unit(1, 2)
    unit(3, 2)
    unit(0, 1)
    came_right(2)
    onward(1, 0)
    came_left(2)
    onward(1, 1)
    onward(2, 0)
    onward(2, 1)
    relay(1, 0)
    relay(3, 0)
    came_far(0)
    unit(2, 0)
    unit(1, 1)
    unit(3, 1)
    relay(0, 1)
    relay(0, 2)
    relay(2, 0)
    for copy in spreads:
        copy.wait_recv()
    for r in (0, 1, 3, 2):
        finish(r, 0)
    relay(1, 1)
    relay(3, 1)
    came_far(1)
    unit(2, 1)
    relay(1, 2)
    relay(3, 2)
    came_far(2)
    unit(2, 2)
    relay(2, 1)
    for r in (0, 1, 3, 2):
        finish(r, 1)
    relay(2, 2)
    for r in (0, 1, 3, 2):
        finish(r, 2)
    for copy in kept:
        copy.wait()
    for r in range(RING):
        for d in range(1, RING):
            ref = back.at[chunk(r, d)]
            remote(ref, ref, out_send.at[r, d], out_recv.at[r, d], device(d, 0)).wait_recv()
    for copy in metas:
        copy.wait_recv()
    for r in range(RING):
        for d in range(RING):
            slot = meta_all[pl.ds(r * 2 * RING + d, 1)]
            value = meta_all[pl.ds(r * 2 * RING + RING + d, 1)]
            matrix[pl.ds((r * RING + PLACE[d]) * slots, slots)] = jnp.where(slot == place, value, 0.0).astype(BF16)

    def mixed(index):
        span = pl.ds(pl.multiple_of(group_of(index) * block, block), block)
        return lax.dot_general(
            matrix[span],
            back[span, columns(index % RING, share)],
            (((0,), (0,)), ((), ())),
            preferred_element_type=F32,
        )

    def deliver(h, span, total):
        share_out[span] = total.astype(BF16)
        shares.append(
            send(share_out.at[span], share_in.at[span], share_send.at[h], share_recv.at[h], owner)
        )

    shares = []
    sum_over_tp(mixed, deliver, last_scratch)
    for copy in shares:
        copy.wait_recv()
    gather.finish()
    for copy in copies:
        copy.wait_send()


def layer(context, weight, residual, places, gain, router, ids, gate, up, down, slots):
    tokens, share = residual.shape
    width, hidden_units = gate.shape
    total = RING * slots
    dma = pltpu.SemaphoreType.DMA
    return pl.pallas_call(
        layer_kernel,
        out_shape=(
            jax.ShapeDtypeStruct((tokens, share), BF16),
            jax.ShapeDtypeStruct((tokens, share), BF16),
        ),
        in_specs=in_vmem(7) + [pl.BlockSpec(memory_space=pl.ANY)] * 3,
        out_specs=tuple(in_vmem(2)),
        scratch_shapes=[
            pltpu.VMEM((RING * total, width // RING), BF16),
            pltpu.VMEM((RING * 2 * RING, tokens), F32),
            pltpu.VMEM((RING * total, tokens), BF16),
            pltpu.VMEM((tokens, share), BF16),
            pltpu.VMEM((tokens, width), BF16),
            pltpu.VMEM((tokens, 128), F32),
            pltpu.VMEM((total, tokens), BF16),
            pltpu.VMEM((total, width + 128), BF16),
            pltpu.VMEM((2 * RING, tokens), F32),
            pltpu.VMEM((RING * total, width + 128), BF16),
            pltpu.VMEM((width, 2 * hidden_units), BF16),
            pltpu.VMEM((RING * hidden_units, width // RING), BF16),
            pltpu.VMEM((RING * total, RING * hidden_units), BF16),
            pltpu.VMEM((RING * total, width // RING), BF16),
        ]
        + sum_scratch(tokens, share)
        + [dma((2, 4, 2))] * 2
        + [dma((8, 2))] * 2
        + [dma((RING,))] * 2
        + [dma((hidden_units // 128 * 16 + 1,))]
        + [dma((RING, 3))] * 6
        + [dma((3, 2))] * 2
        + [dma((RING,))] * 2
        + [dma((RING, 3, RING))] * 2
        + [dma((RING, 3, 2))] * 2
        + [dma((RING, RING))] * 2
        + [dma((2,))] * 2
        + sum_scratch(tokens, share),
        compiler_params=pltpu.CompilerParams(
            collective_id=0, has_side_effects=True, vmem_limit_bytes=VMEM_BYTES
        ),
        name="layer",
    )(context, weight, residual, places, gain, router, ids, gate, up, down)


def slots_of(expert_ids):
    tp, ep = lax.axis_index("tp"), lax.axis_index("ep")
    rows = expert_ids.shape[0]
    mine = tp * RING + (ep // RING + lax.broadcasted_iota(jnp.int32, (1, RING, 1), 1)) % RING
    hit = jnp.any(expert_ids.T[:, None, :] == mine.reshape(1, RING, 1), axis=0)
    upto = (
        lax.broadcasted_iota(jnp.int32, (rows, rows), 0) <= lax.broadcasted_iota(jnp.int32, (rows, rows), 1)
    ).astype(BF16)
    count = jnp.dot(hit.astype(BF16), upto, preferred_element_type=F32)
    places = jnp.where(hit, count - 1.0, -1.0)
    return jnp.concatenate([places, places], axis=0)


def shards(
    context, out_weight, residual, norm_gain, router_weight, expert_ids, w_gate, w_up, w_down
):
    rows = residual.shape[0]
    capacity = min(rows, 2 * rows * expert_ids.shape[1] // router_weight.shape[0])
    share, state = layer(
        context,
        out_weight,
        residual,
        slots_of(expert_ids),
        norm_gain.astype(F32).reshape(-1, 128),
        router_weight,
        expert_ids.T,
        w_gate[0],
        w_up[0],
        w_down[0],
        capacity,
    )
    return (share.astype(F32) + state.astype(F32)).astype(BF16)


def solution(mesh):
    in_specs = (
        P("ep", "tp"),
        P("tp", None),
        P("ep", "tp"),
        P(),
        P(),
        P("ep", None),
        P(("tp", "ep"), None, None),
        P(("tp", "ep"), None, None),
        P(("tp", "ep"), None, None),
    )
    out_specs = P("ep", "tp")
    return jax.shard_map(shards, mesh=mesh, in_specs=in_specs, out_specs=out_specs, check_vma=False)
```
